128 devices in a mesh: blk: 32 (over x, z, core), grp: 4 (over y).
Axes of the slice: x: 4, y: 4, z: 4, core: 2. Of those that a mesh axis runs over, the one named last changes fastest.
Arguments:
- tokens: bfloat16 [2048, 8192], P(('blk', 'grp')), may hold values from -6 to 6
- cotangent: bfloat16 [2048, 8192], P(('blk', 'grp')), may hold values from -6 to 6
- gate_weight: bfloat16 [8192, 4096], P(None, 'blk'), may hold values from -0.0625 to 0.0625
- up_weight: bfloat16 [8192, 4096], P(None, 'blk'), may hold values from -0.0625 to 0.0625
- down_weight: bfloat16 [4096, 8192], P('blk'), may hold values from -0.09375 to 0.09375
- a_gate: bfloat16 [256, 16, 8192], P('blk'), may hold values from -0.0625 to 0.0625
- a_up: bfloat16 [256, 16, 8192], P('blk'), may hold values from -0.0625 to 0.0625
- down_output_factors: bfloat16 [256, 16, 8192], P('blk'), may hold values from -0.375 to 0.375
- b_gate: bfloat16 [256, 16, 4096], P(None, None, 'blk'), may hold values from -0.375 to 0.375
- b_up: bfloat16 [256, 16, 4096], P(None, None, 'blk'), may hold values from -0.375 to 0.375
- a_down: bfloat16 [256, 16, 4096], P(None, None, 'blk'), may hold values from -0.09375 to 0.09375
- tenant_of_row: int32 [2048], replicated, may hold values from 0 to 255, as said below
- adapter_slot: int32 [256], replicated, may hold values from 0 to 255, as said below
Outputs:
- mixed: bfloat16 [2048, 8192], P(('blk', 'grp'))
- input_grad: bfloat16 [2048, 8192], P(('blk', 'grp'))
- grad_a_gate: float32 [256, 16, 8192], P(('blk', 'grp'))
- grad_a_up: float32 [256, 16, 8192], P(('blk', 'grp'))
- grad_b_down: float32 [256, 16, 8192], P(('blk', 'grp'))
- grad_b_gate: float32 [256, 16, 4096], P('grp', None, 'blk')
- grad_b_up: float32 [256, 16, 4096], P('grp', None, 'blk')
- grad_a_down: float32 [256, 16, 4096], P('grp', None, 'blk')
The draws below stay inside these ranges and needn't reach their ends.
Inputs may be any that keep to these rules, and one draw needn't show every extreme that they name: `tenant_of_row`: among the rows held by the devices of one index of grp, for each index b of blk at most 32 rows have tenants whose adapter slot s has s // 8 == b, and for some b exactly 32 do. A permutation: tenant t's factors in a_gate, a_up and down_output_factors, and its gradients of them, stand at index adapter_slot[t].
All inputs are finite; a program needn't handle non-finite values.
Results may differ from the reference program's by a relative error of at most 0.02.
Values may be sent and summed in bfloat16 or wider, within the bound.
No kernel may reach another device: no remote copies, remote signals or barrier semaphores. Data moves between devices by JAX's collectives and lax.ppermute only.
A program may use at most 192 MiB of HBM per device.

```python
import jax
import jax.numpy as jnp
from jax import lax

D = 8192
FF = 4096
RANK = 16
TENANTS = 256
TOK_DEV = 16
TOKENS = 2048
GROUP_ROWS = 512
N_BLK = 32


def tenant_layout(key):
    base_key = jax.random.fold_in(key, 7013)
    slot_perm = jax.random.permutation(jax.random.fold_in(base_key, 1), TENANTS).astype(jnp.int32)
    tenant_at = jnp.argsort(slot_perm, stable=True).astype(jnp.int32)
    blocks = GROUP_ROWS // TOK_DEV
    groups = TOKENS // GROUP_ROWS
    per_owner = TENANTS // blocks
    capacity = 2 * TOK_DEV

    def one_group(group_key):
        sub_keys = jax.random.split(group_key, 4)
        owner_sorting = jax.random.permutation(sub_keys[0], blocks).astype(jnp.int32)
        pair_split = jax.random.randint(sub_keys[1], (blocks // 2,), 0, capacity + 1).astype(jnp.int32)
        pair_split = pair_split.at[0].set(0)
        owner_loads = jnp.zeros((blocks,), jnp.int32).at[owner_sorting[0::2]].set(pair_split)
        owner_loads = owner_loads.at[owner_sorting[1::2]].set(capacity - pair_split)
        bounds = jnp.cumsum(owner_loads).astype(jnp.int32)
        row_owner = jnp.searchsorted(bounds, jnp.arange(GROUP_ROWS, dtype=jnp.int32), side='right').astype(jnp.int32)
        row_owner = row_owner[jax.random.permutation(sub_keys[2], GROUP_ROWS)]
        local_pick = jax.random.randint(sub_keys[3], (GROUP_ROWS,), 0, per_owner).astype(jnp.int32)
        return tenant_at[row_owner * per_owner + local_pick]
    group_keys = jax.random.split(jax.random.fold_in(base_key, 2), groups)
    layout_rows = jax.vmap(one_group)(group_keys)
    layout_rows = layout_rows.reshape(groups, blocks, TOK_DEV).transpose(1, 0, 2).reshape(TOKENS)
    return (layout_rows.astype(jnp.int32), slot_perm)


def draw_tenant_of_row(key, part):
    return tenant_layout(key)[0]


def draw_adapter_slot(key, part):
    return tenant_layout(key)[1]


def block_levels(stream_key, extent, pieces, least, high):
    level, own = 1.0, jax.random.fold_in(stream_key, 6)
    for axis_at, blocks in pieces:
        draws = jnp.exp(jax.random.uniform(jax.random.fold_in(own, axis_at), (blocks,), jnp.float32, least / len(pieces), high / len(pieces)))
        level = level * jnp.repeat(draws, extent[axis_at] // blocks).reshape([-1 if axis == axis_at else 1 for axis in range(len(extent))])
    return level


def centred(rng, extent, width, most, shards=(), kind=jnp.bfloat16):
    loudness = block_levels(rng, extent, shards, -0.22, 0.18) if shards else 1.0
    result = jax.random.normal(rng, extent, jnp.float32) * width * loudness
    return jnp.minimum(jnp.maximum(result, -most), most).astype(kind)


def setup_inputs(seed: int = 0) -> dict:
    streams_of = jax.random.split(jax.random.key(seed), 14)
    tokens = centred(streams_of[0], (TOKENS, D), 1.0, 6.0, ((0, 128),))
    cotangent = centred(streams_of[1], (TOKENS, D), 0.5, 6.0, ((0, 128),))
    gate_weight = centred(streams_of[2], (D, FF), D ** -0.5, 0.0625, ((1, 32),))
    up_weight = centred(streams_of[3], (D, FF), D ** -0.5, 0.0625, ((1, 32),))
    down_weight = centred(streams_of[4], (FF, D), FF ** -0.5, 0.09375, ((0, 32),))
    a_gate = centred(streams_of[5], (TENANTS, RANK, D), D ** -0.5, 0.0625, ((0, 32),))
    a_up = centred(streams_of[6], (TENANTS, RANK, D), D ** -0.5, 0.0625, ((0, 32),))
    down_output_factors = centred(streams_of[7], (TENANTS, RANK, D), (16 * RANK) ** -0.5, 0.375, ((0, 32),))
    b_gate = centred(streams_of[8], (TENANTS, RANK, FF), (16 * RANK) ** -0.5, 0.375, ((2, 32),))
    b_up = centred(streams_of[9], (TENANTS, RANK, FF), (16 * RANK) ** -0.5, 0.375, ((2, 32),))
    a_down = centred(streams_of[10], (TENANTS, RANK, FF), FF ** -0.5, 0.09375, ((2, 32),))
    tenant_of_row = draw_tenant_of_row(jax.random.fold_in(streams_of[13], 71), 0)
    adapter_slot = draw_adapter_slot(jax.random.fold_in(streams_of[13], 71), 0)
    return {"tokens": tokens, "cotangent": cotangent, "gate_weight": gate_weight, "up_weight": up_weight, "down_weight": down_weight, "a_gate": a_gate, "a_up": a_up, "down_output_factors": down_output_factors, "b_gate": b_gate, "b_up": b_up, "a_down": a_down, "tenant_of_row": tenant_of_row, "adapter_slot": adapter_slot}


adapter_scale = 2.0


def silu_pair(gate_in):
    sigmoid_val = jax.nn.sigmoid(gate_in)
    return gate_in * sigmoid_val, sigmoid_val * (1.0 + gate_in * (1.0 - sigmoid_val))


def contract_dims(left_op, right_op, form):
    return jnp.einsum(form, left_op.astype(jnp.float32), right_op.astype(jnp.float32), precision=lax.Precision.HIGHEST)


def round_sum(parts):
    rounded = lax.optimization_barrier(parts.astype(jnp.bfloat16))
    return jnp.sum(rounded.astype(jnp.float32), axis=1).astype(jnp.bfloat16)


def reference(tokens, cotangent, gate_weight, up_weight, down_weight, a_gate, a_up, down_output_factors, b_gate, b_up, a_down, tenant_of_row, adapter_slot):
    per_owner = TENANTS // N_BLK
    unit_width = FF // N_BLK
    block_rows = 128 if TOKENS % 128 == 0 else TOKENS
    num_blocks = TOKENS // block_rows
    slot_of_row = adapter_slot[tenant_of_row].astype(jnp.int32)
    gate_blocks = gate_weight.reshape(D, N_BLK, unit_width)
    up_blocks = up_weight.reshape(D, N_BLK, unit_width)
    down_blocks = down_weight.reshape(N_BLK, unit_width, D)

    def one_block(totals, block_id):
        first_row = (block_id * block_rows).astype(jnp.int32)
        row_x = lax.dynamic_slice_in_dim(tokens, first_row, block_rows, 0)
        row_dy = lax.dynamic_slice_in_dim(cotangent, first_row, block_rows, 0)
        row_slot = lax.dynamic_slice_in_dim(slot_of_row, first_row, block_rows, 0)
        row_tenant = lax.dynamic_slice_in_dim(tenant_of_row.astype(jnp.int32), first_row, block_rows, 0)
        row_owner = row_slot // per_owner
        fac_ag = a_gate[row_slot]
        fac_au = a_up[row_slot]
        fac_bd = down_output_factors[row_slot]
        fac_bg = b_gate[row_tenant]
        fac_bu = b_up[row_tenant]
        fac_ad = a_down[row_tenant]
        p_gate = contract_dims(row_x, fac_ag, "nd,nrd->nr").astype(jnp.bfloat16)
        p_up = contract_dims(row_x, fac_au, "nd,nrd->nr").astype(jnp.bfloat16)
        grad_q = (adapter_scale * contract_dims(row_dy, fac_bd, "nd,nrd->nr")).astype(jnp.bfloat16)
        gate_val = jnp.dot(row_x, gate_weight, preferred_element_type=jnp.float32) + adapter_scale * contract_dims(p_gate, fac_bg, "nr,nrf->nf")
        up_val = jnp.dot(row_x, up_weight, preferred_element_type=jnp.float32) + adapter_scale * contract_dims(p_up, fac_bu, "nr,nrf->nf")
        act_val, act_slope = silu_pair(gate_val)
        hidden = (act_val * up_val).astype(jnp.bfloat16)
        low_q = contract_dims(hidden, fac_ad, "nf,nrf->nr").astype(jnp.bfloat16)
        owner_hot = (row_owner[:, None] == jnp.arange(N_BLK, dtype=jnp.int32)[None, :]).astype(jnp.float32)
        mixed_extra = adapter_scale * contract_dims(low_q, fac_bd, "nr,nrd->nd")
        mixed_parts = contract_dims(hidden.reshape(block_rows, N_BLK, unit_width), down_blocks, "nkf,kfd->nkd") + owner_hot[:, :, None] * mixed_extra[:, None, :]
        mixed_rows = round_sum(mixed_parts)
        grad_h = lax.dot_general(row_dy, down_weight, (((1,), (1,)), ((), ())), preferred_element_type=jnp.float32) + contract_dims(grad_q, fac_ad, "nr,nrf->nf")
        grad_gate = (grad_h * up_val * act_slope).astype(jnp.bfloat16)
        grad_up = (grad_h * act_val).astype(jnp.bfloat16)
        dp_gate = (adapter_scale * contract_dims(grad_gate, fac_bg, "nf,nrf->nr")).astype(jnp.bfloat16)
        dp_up = (adapter_scale * contract_dims(grad_up, fac_bu, "nf,nrf->nr")).astype(jnp.bfloat16)
        input_extra = contract_dims(dp_gate, fac_ag, "nr,nrd->nd") + contract_dims(dp_up, fac_au, "nr,nrd->nd")
        input_parts = contract_dims(grad_gate.reshape(block_rows, N_BLK, unit_width), gate_blocks, "nkf,dkf->nkd")
        input_parts = input_parts + contract_dims(grad_up.reshape(block_rows, N_BLK, unit_width), up_blocks, "nkf,dkf->nkd")
        input_parts = input_parts + owner_hot[:, :, None] * input_extra[:, None, :]
        input_rows = round_sum(input_parts)
        sum_ag = totals[0] + jax.ops.segment_sum(contract_dims(dp_gate, row_x, "nr,nd->nrd"), row_slot, num_segments=TENANTS)
        sum_au = totals[1] + jax.ops.segment_sum(contract_dims(dp_up, row_x, "nr,nd->nrd"), row_slot, num_segments=TENANTS)
        sum_bd = totals[2] + adapter_scale * jax.ops.segment_sum(contract_dims(low_q, row_dy, "nr,nd->nrd"), row_slot, num_segments=TENANTS)
        sum_bg = totals[3] + adapter_scale * jax.ops.segment_sum(contract_dims(p_gate, grad_gate, "nr,nf->nrf"), row_tenant, num_segments=TENANTS)
        sum_bu = totals[4] + adapter_scale * jax.ops.segment_sum(contract_dims(p_up, grad_up, "nr,nf->nrf"), row_tenant, num_segments=TENANTS)
        sum_ad = totals[5] + jax.ops.segment_sum(contract_dims(grad_q, hidden, "nr,nf->nrf"), row_tenant, num_segments=TENANTS)
        return (sum_ag, sum_au, sum_bd, sum_bg, sum_bu, sum_ad), (mixed_rows, input_rows)

    zeros_d = jnp.zeros((TENANTS, RANK, D), jnp.float32)
    zero_feature_block = jnp.zeros((TENANTS, RANK, FF), jnp.float32)
    totals, stacked = lax.scan(one_block, (zeros_d, zeros_d, zeros_d, zero_feature_block, zero_feature_block, zero_feature_block), jnp.arange(num_blocks, dtype=jnp.int32))
    mixed = stacked[0].reshape(TOKENS, D)
    input_grad = stacked[1].reshape(TOKENS, D)
    return (mixed, input_grad, totals[0], totals[1], totals[2], totals[3], totals[4], totals[5])
```

```python
import jax
import jax.numpy as jnp
from jax import lax
from jax.experimental import pallas as pl
from jax.experimental.pallas import tpu as pltpu
from jax.sharding import Mesh
from jax.sharding import PartitionSpec as P

RING = 4
CORES = 2
BLK = ("x", "z", "c")
UP = [(i, (i + 1) % RING) for i in range(RING)]
DOWN = [(i, (i - 1) % RING) for i in range(RING)]
SWAP = [(0, 1), (1, 0)]
RANK = 16
LANES = 128
BF = jnp.bfloat16
F32 = jnp.float32


def params(mib):
    return pltpu.CompilerParams(vmem_limit_bytes=mib << 20)


def dot(a, b):
    return jnp.dot(a, b, preferred_element_type=F32)


def dot_nt(a, b):
    return lax.dot_general(a, b, (((1,), (1,)), ((), ())), preferred_element_type=F32)


def iota(shape, dim):
    return lax.broadcasted_iota(jnp.int32, shape, dim)


def folding(rows, first):
    return ((iota((rows, LANES), 0) & 15) + first == iota((rows, LANES), 1)).astype(BF)


def tiling(first, cols):
    return (iota((LANES, cols), 0) == (iota((LANES, cols), 1) & 15) + first).astype(BF)


def project_kernel(
    rel, choose, x, dy, gate_w, up_w, down_w, a_g, a_u, out_f, pre, coef, own, acc_x, acc_dy
):
    j = pl.program_id(0)

    @pl.when(j == 0)
    def _():
        acc_x[...] = jnp.zeros_like(acc_x)
        acc_dy[...] = jnp.zeros_like(acc_dy)

    xv, dv = x[...], dy[...]
    acc_x[:, : 2 * LANES] += dot(xv, jnp.concatenate([gate_w[...], up_w[...]], axis=1))
    acc_x[:, 2 * LANES :] += dot_nt(xv, jnp.concatenate([a_g[...], a_u[...]], axis=0))
    acc_dy[...] += dot_nt(dv, jnp.concatenate([down_w[...], out_f[...]], axis=0))
    cap = choose.shape[0]
    own[:cap, :] = dot(choose[...], xv).astype(BF)
    own[cap:, :] = dot(choose[...], dv).astype(BF)

    @pl.when(j == pl.num_programs(0) - 1)
    def _():
        pre[:, : 2 * LANES] = acc_x[:, : 2 * LANES]
        pre[:, 2 * LANES :] = acc_dy[:, :LANES]
        rows = xv.shape[0]
        mine = rel[...] == (iota((rows, LANES), 1) >> 4)
        zero = jnp.zeros((rows, LANES), F32)
        z_g = jnp.where(mine, acc_x[:, 2 * LANES : 3 * LANES], zero).astype(BF)
        z_u = jnp.where(mine, acc_x[:, 3 * LANES :], zero).astype(BF)
        z_q = jnp.where(mine, 2.0 * acc_dy[:, LANES:], zero).astype(BF)
        packed = (
            dot(z_g, folding(LANES, 0))
            + dot(z_u, folding(LANES, RANK))
            + dot(z_q, folding(LANES, 2 * RANK))
        )
        coef[...] = dot(choose[...], packed.astype(BF)).astype(BF)


def project(rel, choose, both, gate_w, up_w, down_w, a_g, a_u, out_f):
    rows, d = both.shape[0], both.shape[1] // 2
    cap = choose.shape[0]
    width = 1024
    steps = d // width
    tall = pl.BlockSpec((width, LANES), lambda j: (j, 0))
    wide = pl.BlockSpec((LANES, width), lambda j: (0, j))
    return pl.pallas_call(
        project_kernel,
        grid=(steps,),
        in_specs=[
            pl.BlockSpec((rows, 1), lambda j: (0, 0)),
            pl.BlockSpec((cap, rows), lambda j: (0, 0)),
            pl.BlockSpec((rows, width), lambda j: (0, j)),
            pl.BlockSpec((rows, width), lambda j: (0, j + steps)),
            tall,
            tall,
            wide,
            wide,
            wide,
            wide,
        ],
        out_specs=[
            pl.BlockSpec((rows, 3 * LANES), lambda j: (0, 0)),
            pl.BlockSpec((cap, LANES), lambda j: (0, 0)),
            pl.BlockSpec((2 * cap, width), lambda j: (0, j)),
        ],
        out_shape=[
            jax.ShapeDtypeStruct((rows, 3 * LANES), F32),
            jax.ShapeDtypeStruct((cap, LANES), BF),
            jax.ShapeDtypeStruct((2 * cap, d), BF),
        ],
        scratch_shapes=[pltpu.VMEM((rows, 4 * LANES), F32), pltpu.VMEM((rows, 2 * LANES), F32)],
        compiler_params=params(32),
        name="project",
    )(rel, choose, both, both, gate_w, up_w, down_w, a_g, a_u, out_f)


def hidden_kernel(tenant, pos, pos_row, table, pre, b_g, b_u, a_d, values, placed, partial):
    j = pl.program_id(0)
    rows = pre.shape[0]
    wide = 512
    spots = table.shape[0]
    here = (pos[...] == iota((rows, spots), 1)).astype(BF)
    coefs = dot(here, table[...]).astype(BF)
    tiles = [dot(coefs, tiling(k * RANK, wide)) for k in range(3)]
    who = tenant[...]
    extra = [jnp.zeros((rows, LANES), F32) for _ in range(3)]
    factors = (b_g, b_u, a_d)
    count = b_g.shape[0] // wide
    lane_tenant = iota((rows, wide), 1) >> 4
    for k in range(count):
        mine = (who - k * (wide // RANK)) == lane_tenant
        for m in range(3):
            e = jnp.where(mine, tiles[m], 0.0).astype(BF)
            extra[m] += dot(e, factors[m][k * wide : (k + 1) * wide, :])
    gate = pre[:, :LANES] + 2.0 * extra[0]
    up = pre[:, LANES : 2 * LANES] + 2.0 * extra[1]
    grad = pre[:, 2 * LANES :] + extra[2]
    sig = 1.0 / (1.0 + jnp.exp(-gate))
    act = gate * sig
    slope = sig * (1.0 + gate * (1.0 - sig))
    hidden = (act * up).astype(BF)
    grad_gate = (grad * up * slope).astype(BF)
    grad_up = (grad * act).astype(BF)
    values[:, :LANES] = hidden
    values[:, LANES : 2 * LANES] = grad_gate
    values[:, 2 * LANES : 3 * LANES] = grad_up
    values[:, 3 * LANES :] = coefs
    low = jnp.zeros((rows, LANES), F32)
    for left, right, first, scale in (
        (hidden, a_d, 0, 1.0),
        (grad_gate, b_g, RANK, 2.0),
        (grad_up, b_u, 2 * RANK, 2.0),
    ):
        total = jnp.zeros((rows, wide), F32)
        for k in range(count):
            mine = (who - k * (wide // RANK)) == lane_tenant
            z = dot_nt(left, right[k * wide : (k + 1) * wide, :])
            total = jnp.where(mine, z, total)
        low += dot((scale * total).astype(BF), folding(wide, first))
    partial[pl.ds(pl.multiple_of(j * rows, rows), rows), :] = low.astype(BF)

    @pl.when(j == pl.num_programs(0) - 1)
    def _():
        every = partial.shape[0]
        put = (pos_row[...] == iota((spots, every), 0)).astype(BF)
        placed[...] = dot(put, partial[...]).astype(BF)


def hidden_stage(tenant, pos, pos_row, table, pre, b_g, b_u, a_d):
    rows = pre.shape[0]
    part = 128
    whole = lambda a: pl.BlockSpec(a.shape, lambda j: (0, 0))
    spots = table.shape[0]
    return pl.pallas_call(
        hidden_kernel,
        grid=(rows // part,),
        in_specs=[
            pl.BlockSpec((part, 1), lambda j: (j, 0)),
            pl.BlockSpec((part, 1), lambda j: (j, 0)),
            whole(pos_row),
            whole(table),
            pl.BlockSpec((part, 3 * LANES), lambda j: (j, 0)),
            whole(b_g),
            whole(b_u),
            whole(a_d),
        ],
        out_specs=[
            pl.BlockSpec((part, 4 * LANES), lambda j: (j, 0)),
            pl.BlockSpec((spots, LANES), lambda j: (0, 0)),
        ],
        out_shape=[
            jax.ShapeDtypeStruct((rows, 4 * LANES), BF),
            jax.ShapeDtypeStruct((spots, LANES), BF),
        ],
        scratch_shapes=[pltpu.VMEM((rows, LANES), BF)],
        compiler_params=params(40),
        name="hidden_stage",
    )(tenant, pos, pos_row, table, pre, b_g, b_u, a_d)


def left_kernel(rel, choose_t, low, order_m, order_i, values, left):
    rows = rel.shape[0]
    mine = rel[...] == (iota((rows, LANES), 1) >> 4)
    back = dot(choose_t[...], low[...]).astype(BF)
    spread = lambda first, scale: jnp.where(
        mine, scale * dot(back, tiling(first, LANES)), 0.0
    ).astype(BF)
    for_mixed = jnp.concatenate([values[:, :LANES], spread(0, 2.0)], axis=1)
    for_input = jnp.concatenate(
        [values[:, LANES : 3 * LANES], spread(RANK, 1.0), spread(2 * RANK, 1.0)], axis=1
    )
    at = iota((rows, rows), 1)
    left[:, : 2 * LANES] = dot((order_m[...] == at).astype(BF), for_mixed).astype(BF)
    left[:, 2 * LANES :] = dot((order_i[...] == at).astype(BF), for_input).astype(BF)


def left_stage(rel, choose_t, low, order_m, order_i, values):
    rows = rel.shape[0]
    return pl.pallas_call(
        left_kernel,
        out_shape=jax.ShapeDtypeStruct((rows, 6 * LANES), BF),
        compiler_params=params(40),
        name="left_stage",
    )(rel, choose_t, low, order_m, order_i, values)


def product_kernel(core, left, other, down_w, out_f, gate_w, up_w, a_g, a_u, near, side, *outs):
    del core
    m, i = 2 * LANES, 4 * LANES
    total = dot(left[:, :m], jnp.concatenate([down_w[...], out_f[...]], axis=0))
    total += dot(other[:, :m], near[:m, :])
    mixed = total.astype(BF)
    total = dot_nt(left[:, m:i], jnp.concatenate([gate_w[...], up_w[...]], axis=1))
    total += dot(left[:, i:], jnp.concatenate([a_g[...], a_u[...]], axis=0))
    total += dot_nt(other[:, m:i], side[...])
    total += dot(other[:, i:], near[m:, :])
    back = total.astype(BF)
    n = mixed.shape[0] // 4
    h = n // 2
    for at, value in ((0, mixed), (7, back)):
        for k, (first, count) in enumerate(
            ((0, n), (n, h), (n + h, h), (2 * n, h), (2 * n + h, h), (3 * n, h), (3 * n + h, h))
        ):
            outs[at + k][...] = value[first : first + count, :]


def products(core, left, other, down_w, out_f, gate_w, up_w, a_g, a_u, near, side):
    rows, half = left.shape[0], near.shape[1]
    width = 512
    steps = half // width
    n = rows // 4
    whole = lambda a: pl.BlockSpec(a.shape, lambda j, c: (0, 0))
    wide = pl.BlockSpec((LANES, width), lambda j, c: (0, c[0] * steps + j))
    tall = pl.BlockSpec((width, LANES), lambda j, c: (c[0] * steps + j, 0))
    counts = 2 * [n, n // 2, n // 2, n // 2, n // 2, n // 2, n // 2]
    return pl.pallas_call(
        product_kernel,
        grid_spec=pltpu.PrefetchScalarGridSpec(
            num_scalar_prefetch=1,
            grid=(steps,),
            in_specs=[
                whole(left),
                whole(other),
                wide,
                wide,
                tall,
                tall,
                wide,
                wide,
                pl.BlockSpec((near.shape[0], width), lambda j, c: (0, j)),
                pl.BlockSpec((width, side.shape[1]), lambda j, c: (j, 0)),
            ],
            out_specs=[pl.BlockSpec((k, width), lambda j, c: (0, j)) for k in counts],
        ),
        out_shape=[jax.ShapeDtypeStruct((k, half), BF) for k in counts],
        compiler_params=params(40),
        name="products",
    )(core, left, other, down_w, out_f, gate_w, up_w, a_g, a_u, near, side)


def tenant_kernel(rel_tenant, values, out_bg, out_bu, out_ad):
    groups = rel_tenant.shape[0]
    some = 256
    rows = rel_tenant.shape[1]
    sub = iota((some, rows), 0)
    for out, left, first, scale in (
        (out_bg, 1, 0, 2.0),
        (out_bu, 2, RANK, 2.0),
        (out_ad, 0, 2 * RANK, 1.0),
    ):
        pick = (iota((some, LANES), 1) == (iota((some, LANES), 0) & 15) + first).astype(BF)
        sums = [jnp.zeros((some, LANES), F32) for _ in range(out.shape[0] // some)]
        for g in range(groups):
            tile = dot_nt(pick, values[g, :rows, 3 * LANES :])
            rhs = values[g, :rows, left * LANES : (left + 1) * LANES]
            who = rel_tenant[g : g + 1, :]
            for k in range(len(sums)):
                mine = (who - k * (some // RANK)) == (sub >> 4)
                sums[k] += dot(jnp.where(mine, tile, 0.0).astype(BF), rhs)
        for k, total in enumerate(sums):
            out[k * some : (k + 1) * some, :] = scale * total


def tenant_gradients(rel_tenant, values, tenants):
    shape = jax.ShapeDtypeStruct((tenants * RANK, LANES), F32)
    return pl.pallas_call(
        tenant_kernel,
        out_shape=[shape] * 3,
        compiler_params=params(40),
        name="tenant_gradients",
    )(rel_tenant, values)


def slot_kernel(weights, own, out_g, out_u, out_d):
    groups, cap = own.shape[0], own.shape[1] // 2
    x = jnp.concatenate([own[g, :cap, :] for g in range(groups)], axis=0)
    dy = jnp.concatenate([own[g, cap:, :] for g in range(groups)], axis=0)
    n = out_g.shape[0]
    both = dot(weights[: 2 * n, :], x)
    out_g[...] = both[:n, :]
    out_u[...] = both[n:, :]
    out_d[...] = dot(weights[2 * n :, :], dy)


def slot_gradients(weights, own):
    groups, rows, d = own.shape
    n = weights.shape[0] // 3
    width = 1024
    spec = pl.BlockSpec((n, width), lambda j: (0, j))
    return pl.pallas_call(
        slot_kernel,
        grid=(d // width,),
        in_specs=[
            pl.BlockSpec(weights.shape, lambda j: (0, 0)),
            pl.BlockSpec((groups, rows, width), lambda j: (0, 0, j)),
        ],
        out_specs=[spec] * 3,
        out_shape=[jax.ShapeDtypeStruct((n, d), F32)] * 3,
        compiler_params=params(32),
        name="slot_gradients",
    )(weights, own)


def add(*terms):
    total = terms[0].astype(F32)
    for t in terms[1:]:
        total = total + t.astype(F32)
    return total.astype(BF)


def first_step(a, b, axes, *beside):
    sent = []
    for p, axis in ((a, axes[0]), (b, axes[1])):
        sent += [lax.ppermute(p[3], axis, UP), lax.ppermute(p[4], axis, DOWN)]
    done = lax.optimization_barrier((*sent, *beside))
    return done[:4], done[4:]


def second_start(a, b, axes, sent):
    moved = []
    for k, (p, axis) in enumerate(((a, axes[0]), (b, axes[1]))):
        right = jnp.concatenate([add(p[1], sent[2 * k]), p[2]], axis=0)
        left = jnp.concatenate([p[5], add(p[6], sent[2 * k + 1])], axis=0)
        moved += [lax.ppermute(right, axis, UP), lax.ppermute(left, axis, DOWN)]
    return moved


def second_end(a, b, moved, *beside):
    done = lax.optimization_barrier((*moved, *beside))
    moved, beside = done[:4], done[4:]
    return add(a[0], moved[0], moved[1]), add(b[0], moved[2], moved[3]), beside


def ring_near(v, axis):
    return lax.ppermute(v, axis, UP), lax.ppermute(v, axis, DOWN)


def ring_far(left, right, axis):
    h = left.shape[0] // 2
    return lax.ppermute(left[:h], axis, UP), lax.ppermute(right[h:], axis, DOWN)


def ring_join(v, near, far):
    return jnp.stack([v, *near, jnp.concatenate(far, axis=0)], axis=0)


def sevenths(v):
    n = v.shape[0] // 4
    h = n // 2
    cut = lambda first, count: v[first : first + count]
    return (
        cut(0, n),
        cut(n, h),
        cut(n + h, h),
        cut(2 * n, h),
        cut(2 * n + h, h),
        cut(3 * n, h),
        cut(3 * n + h, h),
    )


def local(
    tokens,
    cotangent,
    gate_weight,
    up_weight,
    down_weight,
    a_gate,
    a_up,
    down_output_factors,
    b_gate,
    b_up,
    a_down,
    tenant_of_row,
    adapter_slot,
):
    own_rows, d = tokens.shape
    half = d // CORES
    blk_count = lax.axis_size(BLK)
    grp_count = lax.axis_size("y")
    x_at, z_at, c_at, grp = (lax.axis_index(k) for k in ("x", "z", "c", "y"))
    blk = (x_at * RING + z_at) * CORES + c_at
    per_owner = a_gate.shape[0]
    tenant_count = b_gate.shape[0]
    cap = 2 * own_rows
    group_rows = own_rows * blk_count

    a_g = a_gate.reshape(per_owner * RANK, d)
    a_u = a_up.reshape(per_owner * RANK, d)
    out_f = down_output_factors.reshape(per_owner * RANK, d)
    b_g = b_gate.reshape(tenant_count * RANK, -1)
    b_u = b_up.reshape(tenant_count * RANK, -1)
    a_d = a_down.reshape(tenant_count * RANK, -1)

    all_tenants = jnp.transpose(tenant_of_row.reshape(blk_count, grp_count, own_rows), (1, 0, 2))
    all_tenants = all_tenants.reshape(grp_count, group_rows)
    hot = all_tenants[:, :, None] == jnp.arange(tenant_count, dtype=jnp.int32)
    all_slots = jnp.sum(jnp.where(hot, adapter_slot, 0), axis=2)
    all_owners = all_slots // per_owner
    at = jnp.arange(group_rows, dtype=jnp.int32)
    ahead = (all_owners[:, :, None] == all_owners[:, None, :]) & (at[:, None] > at[None, :])
    all_within = jnp.sum(ahead.astype(jnp.int32), axis=2)
    mine = all_owners == blk
    all_choose = mine[:, None, :] & (
        all_within[:, None, :] == jnp.arange(cap, dtype=jnp.int32)[None, :, None]
    )
    own_slot = jnp.sum(jnp.where(all_choose, (all_slots - per_owner * blk)[:, None, :] + 1, 0), 2) - 1
    here = lambda v: lax.dynamic_index_in_dim(v, grp, 0, keepdims=False)
    tenants, slots = here(all_tenants), here(all_slots)
    position = here(all_owners) * cap + here(all_within)
    choose = here(all_choose).astype(BF)
    rel = slots - per_owner * blk

    far = (1 - c_at) * half
    cut_wide = lambda v: lax.dynamic_slice_in_dim(v, far, half, 1)
    cut_tall = lambda v: lax.dynamic_slice_in_dim(v, far, half, 0)
    near = jnp.concatenate([cut_wide(v) for v in (down_weight, out_f, a_g, a_u)], axis=0)
    side = jnp.concatenate([cut_tall(gate_weight), cut_tall(up_weight)], axis=1)
    near = lax.ppermute(near, "c", SWAP)
    side = lax.ppermute(side, "c", SWAP)

    j = jnp.arange(group_rows, dtype=jnp.int32)
    inner = j % (CORES * own_rows)
    first, second = j // (group_rows // RING), (j // (CORES * own_rows)) % RING
    place = lambda dx, dz: (
        ((x_at + dx) % RING * RING + (z_at + dz) % RING) * CORES * own_rows + inner
    )[:, None]
    order_m, order_i = place(first, second), place(second, first)

    both = jnp.concatenate([tokens, cotangent], axis=1)
    both = lax.all_gather(both, BLK, axis=0, tiled=True)
    rel = rel[:, None]
    pre, coef, own = project(
        rel, choose, both, gate_weight, up_weight, down_weight, a_g, a_u, out_f
    )
    own_near = ring_near(own, "y")
    copies = jnp.broadcast_to(coef[:, : 3 * RANK], (blk_count, cap, 3 * RANK))
    table = lax.all_to_all(copies, BLK, split_axis=0, concat_axis=0, tiled=True)
    table = jnp.pad(table.reshape(blk_count * cap, 3 * RANK), ((0, 0), (0, LANES - 3 * RANK)))
    values, placed = hidden_stage(
        tenants[:, None], position[:, None], position[None, :], table, pre, b_g, b_u, a_d
    )
    placed, *own_near = lax.optimization_barrier((placed, *own_near))
    own_far = ring_far(*own_near, "y")
    terms = placed[:, : 3 * RANK].reshape(blk_count, cap, 3 * RANK)
    terms = lax.all_to_all(terms, BLK, split_axis=0, concat_axis=0, tiled=True)
    low = jnp.sum(terms.astype(F32), axis=0).astype(BF)
    low = jnp.pad(low, ((0, cap), (0, LANES - 3 * RANK)))
    left = left_stage(rel, jnp.transpose(choose), low[:cap], order_m, order_i, values)
    other = lax.ppermute(left, "c", SWAP)
    packed = jnp.concatenate([values, low.reshape(-1, 4 * LANES)], axis=0)
    left, other, packed, *own_far = lax.optimization_barrier((left, other, packed, *own_far))
    packed_near = ring_near(packed, "y")
    pieces = products(
        c_at.reshape(1).astype(jnp.int32),
        left,
        other,
        down_weight,
        out_f,
        gate_weight,
        up_weight,
        a_g,
        a_u,
        near,
        side,
    )
    pieces = (pieces[:7], pieces[7:])
    sent, packed_near = first_step(*pieces, ("x", "z"), *packed_near)
    moved = second_start(*pieces, ("x", "z"), sent)
    packed_far = ring_far(*packed_near, "y")

    all_own = ring_join(own, own_near, own_far)
    packed = ring_join(packed, packed_near, packed_far)
    turn = (grp + jnp.array([0, -1, 1, 2], jnp.int32)) % grp_count
    turned = lambda v: jnp.sum(
        jnp.where((turn[:, None] == jnp.arange(grp_count, dtype=jnp.int32))[:, :, None], v[None], 0), 1
    )
    low_all = packed[:, group_rows:, :].astype(F32)
    low_all = low_all.reshape(grp_count, -1, LANES)[:, :cap, : 3 * RANK]
    slots_dev = per_owner // grp_count
    wanted = grp * slots_dev + jnp.arange(slots_dev, dtype=jnp.int32)
    weights = jnp.where(
        (turned(own_slot)[None] == wanted[:, None, None])[:, None],
        jnp.transpose(low_all, (2, 0, 1))[None],
        0.0,
    )
    weights = weights.reshape(slots_dev, 3, RANK, grp_count * cap)
    weights = jnp.transpose(weights, (1, 0, 2, 3)).reshape(3, slots_dev * RANK, grp_count * cap)
    weights = jnp.concatenate([weights[1], weights[2], 2.0 * weights[0]], axis=0).astype(BF)
    by_slot = slot_gradients(weights, all_own)
    tenant_dev = tenant_count // grp_count
    by_tenant = tenant_gradients(turned(all_tenants) - grp * tenant_dev, packed, tenant_dev)

    *sums, grads = second_end(*pieces, moved, *by_slot, *by_tenant)
    pieces = (sevenths(sums[0]), sevenths(sums[1]))
    sent, _ = first_step(*pieces, ("z", "x"))
    moved = second_start(*pieces, ("z", "x"), sent)
    *sums, _ = second_end(*pieces, moved)
    stacked = jnp.stack([v.reshape(CORES, own_rows, half) for v in sums], axis=1)
    keep = lax.dynamic_index_in_dim(stacked, c_at, 0, keepdims=False)
    give = lax.dynamic_index_in_dim(stacked, 1 - c_at, 0, keepdims=False)
    take = lax.ppermute(give, "c", SWAP)
    result = jnp.where(
        c_at == 0,
        jnp.concatenate([keep, take], axis=2),
        jnp.concatenate([take, keep], axis=2),
    )
    return (
        result[0],
        result[1],
        *(v.reshape(slots_dev, RANK, d) for v in grads[:3]),
        *(v.reshape(tenant_dev, RANK, -1) for v in grads[3:]),
    )


def solution(mesh):
    cut = Mesh(mesh.devices.reshape(RING, RING, CORES, mesh.shape["grp"]), ("x", "z", "c", "y"))
    every = (*BLK, "y")
    return jax.shard_map(
        local,
        mesh=cut,
        in_specs=(
            P(every, None),
            P(every, None),
            P(None, BLK),
            P(None, BLK),
            P(BLK, None),
            P(BLK, None, None),
            P(BLK, None, None),
            P(BLK, None, None),
            P(None, None, BLK),
            P(None, None, BLK),
            P(None, None, BLK),
            P(),
            P(),
        ),
        out_specs=(
            P(every, None),
            P(every, None),
            P(every, None, None),
            P(every, None, None),
            P(every, None, None),
            P("y", None, BLK),
            P("y", None, BLK),
            P("y", None, BLK),
        ),
        check_vma=False,
    )
```

```python
import jax
import jax.numpy as jnp
from jax import lax
from jax.experimental import pallas as pl
from jax.experimental.pallas import tpu as pltpu
from jax.sharding import Mesh
from jax.sharding import PartitionSpec as P

RING = 4
CORES = 2
BLK = ("x", "z", "c")
UP = [(i, (i + 1) % RING) for i in range(RING)]
DOWN = [(i, (i - 1) % RING) for i in range(RING)]
SWAP = [(0, 1), (1, 0)]
RANK = 16
LANES = 128
BF = jnp.bfloat16
F32 = jnp.float32


def params(mib):
    return pltpu.CompilerParams(vmem_limit_bytes=mib << 20)


def dot(a, b):
    return jnp.dot(a, b, preferred_element_type=F32)


def dot_nt(a, b):
    return lax.dot_general(a, b, (((1,), (1,)), ((), ())), preferred_element_type=F32)


def iota(shape, dim):
    return lax.broadcasted_iota(jnp.int32, shape, dim)


def folding(rows, first):
    return ((iota((rows, LANES), 0) & 15) + first == iota((rows, LANES), 1)).astype(BF)


def tiling(first, cols):
    return (iota((LANES, cols), 0) == (iota((LANES, cols), 1) & 15) + first).astype(BF)


def project_kernel(
    rel, choose, x, dy, tall_w, wide_w, pre, coef, own, acc_x, acc_dy
):
    j = pl.program_id(0)

    @pl.when(j == 0)
    def _():
        acc_x[...] = jnp.zeros_like(acc_x)
        acc_dy[...] = jnp.zeros_like(acc_dy)

    xv, dv = x[...], dy[...]
    acc_x[:, : 2 * LANES] += dot(xv, tall_w[...])
    acc_x[:, 2 * LANES :] += dot_nt(xv, wide_w[2 * LANES :, :])
    acc_dy[...] += dot_nt(dv, wide_w[: 2 * LANES, :])
    cap = choose.shape[0]
    own[:cap, :] = dot(choose[...], xv).astype(BF)
    own[cap:, :] = dot(choose[...], dv).astype(BF)

    @pl.when(j == pl.num_programs(0) - 1)
    def _():
        pre[:, : 2 * LANES] = acc_x[:, : 2 * LANES]
        pre[:, 2 * LANES :] = acc_dy[:, :LANES]
        rows = xv.shape[0]
        mine = rel[...] == (iota((rows, LANES), 1) >> 4)
        zero = jnp.zeros((rows, LANES), F32)
        z_g = jnp.where(mine, acc_x[:, 2 * LANES : 3 * LANES], zero).astype(BF)
        z_u = jnp.where(mine, acc_x[:, 3 * LANES :], zero).astype(BF)
        z_q = jnp.where(mine, 2.0 * acc_dy[:, LANES:], zero).astype(BF)
        packed = (
            dot(z_g, folding(LANES, 0))
            + dot(z_u, folding(LANES, RANK))
            + dot(z_q, folding(LANES, 2 * RANK))
        )
        coef[...] = dot(choose[...], packed.astype(BF)).astype(BF)


def project(rel, choose, both, tall_w, wide_w):
    rows, d = both.shape[0], both.shape[1] // 2
    cap = choose.shape[0]
    width = 1024
    steps = d // width
    return pl.pallas_call(
        project_kernel,
        grid=(steps,),
        in_specs=[
            pl.BlockSpec((rows, 1), lambda j: (0, 0)),
            pl.BlockSpec((cap, rows), lambda j: (0, 0)),
            pl.BlockSpec((rows, width), lambda j: (0, j)),
            pl.BlockSpec((rows, width), lambda j: (0, j + steps)),
            pl.BlockSpec((width, tall_w.shape[1]), lambda j: (j, 0)),
            pl.BlockSpec((wide_w.shape[0], width), lambda j: (0, j)),
        ],
        out_specs=[
            pl.BlockSpec((rows, 3 * LANES), lambda j: (0, 0)),
            pl.BlockSpec((cap, LANES), lambda j: (0, 0)),
            pl.BlockSpec((2 * cap, width), lambda j: (0, j)),
        ],
        out_shape=[
            jax.ShapeDtypeStruct((rows, 3 * LANES), F32),
            jax.ShapeDtypeStruct((cap, LANES), BF),
            jax.ShapeDtypeStruct((2 * cap, d), BF),
        ],
        scratch_shapes=[pltpu.VMEM((rows, 4 * LANES), F32), pltpu.VMEM((rows, 2 * LANES), F32)],
        compiler_params=params(32),
        name="project",
    )(rel, choose, both, both, tall_w, wide_w)


def hidden_kernel(tenant, pos, pos_row, table, pre, b_g, b_u, a_d, values, placed, partial):
    j = pl.program_id(0)
    rows = pre.shape[0]
    wide = 512
    spots = table.shape[0]
    here = (pos[...] == iota((rows, spots), 1)).astype(BF)
    coefs = dot(here, table[...]).astype(BF)
    tiles = [dot(coefs, tiling(k * RANK, wide)) for k in range(3)]
    who = tenant[...]
    extra = [jnp.zeros((rows, LANES), F32) for _ in range(3)]
    factors = (b_g, b_u, a_d)
    count = b_g.shape[0] // wide
    lane_tenant = iota((rows, wide), 1) >> 4
    for k in range(count):
        mine = (who - k * (wide // RANK)) == lane_tenant
        for m in range(3):
            e = jnp.where(mine, tiles[m], 0.0).astype(BF)
            extra[m] += dot(e, factors[m][k * wide : (k + 1) * wide, :])
    gate = pre[:, :LANES] + 2.0 * extra[0]
    up = pre[:, LANES : 2 * LANES] + 2.0 * extra[1]
    grad = pre[:, 2 * LANES :] + extra[2]
    sig = 1.0 / (1.0 + jnp.exp(-gate))
    act = gate * sig
    slope = sig * (1.0 + gate * (1.0 - sig))
    hidden = (act * up).astype(BF)
    grad_gate = (grad * up * slope).astype(BF)
    grad_up = (grad * act).astype(BF)
    values[:, :LANES] = hidden
    values[:, LANES : 2 * LANES] = grad_gate
    values[:, 2 * LANES : 3 * LANES] = grad_up
    values[:, 3 * LANES :] = coefs
    low = jnp.zeros((rows, LANES), F32)
    for left, right, first, scale in (
        (hidden, a_d, 0, 1.0),
        (grad_gate, b_g, RANK, 2.0),
        (grad_up, b_u, 2 * RANK, 2.0),
    ):
        total = jnp.zeros((rows, wide), F32)
        for k in range(count):
            mine = (who - k * (wide // RANK)) == lane_tenant
            z = dot_nt(left, right[k * wide : (k + 1) * wide, :])
            total = jnp.where(mine, z, total)
        low += dot((scale * total).astype(BF), folding(wide, first))
    partial[pl.ds(pl.multiple_of(j * rows, rows), rows), :] = low.astype(BF)

    @pl.when(j == pl.num_programs(0) - 1)
    def _():
        every = partial.shape[0]
        put = (pos_row[...] == iota((spots, every), 0)).astype(BF)
        placed[...] = dot(put, partial[...]).astype(BF)


def hidden_stage(tenant, pos, pos_row, table, pre, b_g, b_u, a_d):
    rows = pre.shape[0]
    part = 256
    whole = lambda a: pl.BlockSpec(a.shape, lambda j: (0, 0))
    spots = table.shape[0]
    return pl.pallas_call(
        hidden_kernel,
        grid=(rows // part,),
        in_specs=[
            pl.BlockSpec((part, 1), lambda j: (j, 0)),
            pl.BlockSpec((part, 1), lambda j: (j, 0)),
            whole(pos_row),
            whole(table),
            pl.BlockSpec((part, 3 * LANES), lambda j: (j, 0)),
            whole(b_g),
            whole(b_u),
            whole(a_d),
        ],
        out_specs=[
            pl.BlockSpec((part, 4 * LANES), lambda j: (j, 0)),
            pl.BlockSpec((spots, LANES), lambda j: (0, 0)),
        ],
        out_shape=[
            jax.ShapeDtypeStruct((rows, 4 * LANES), BF),
            jax.ShapeDtypeStruct((spots, LANES), BF),
        ],
        scratch_shapes=[pltpu.VMEM((rows, LANES), BF)],
        compiler_params=params(40),
        name="hidden_stage",
    )(tenant, pos, pos_row, table, pre, b_g, b_u, a_d)


def left_kernel(rel, choose_t, low, order_m, order_i, values, left):
    rows = rel.shape[0]
    mine = rel[...] == (iota((rows, LANES), 1) >> 4)
    back = dot(choose_t[...], low[...]).astype(BF)
    spread = lambda first, scale: jnp.where(
        mine, scale * dot(back, tiling(first, LANES)), 0.0
    ).astype(BF)
    for_mixed = jnp.concatenate([values[:, :LANES], spread(0, 2.0)], axis=1)
    for_input = jnp.concatenate(
        [values[:, LANES : 3 * LANES], spread(RANK, 1.0), spread(2 * RANK, 1.0)], axis=1
    )
    at = iota((rows, rows), 1)
    left[:, : 2 * LANES] = dot((order_m[...] == at).astype(BF), for_mixed).astype(BF)
    left[:, 2 * LANES :] = dot((order_i[...] == at).astype(BF), for_input).astype(BF)


def left_stage(rel, choose_t, low, order_m, order_i, values):
    rows = rel.shape[0]
    return pl.pallas_call(
        left_kernel,
        out_shape=jax.ShapeDtypeStruct((rows, 6 * LANES), BF),
        compiler_params=params(40),
        name="left_stage",
    )(rel, choose_t, low, order_m, order_i, values)


def product_kernel(core, left, other, tall_w, wide_w, near, side, *outs):
    del core
    m, i = 2 * LANES, 4 * LANES
    total = dot(left[:, :m], wide_w[:m, :])
    total += dot(other[:, :m], near[:m, :])
    mixed = total.astype(BF)
    total = dot_nt(left[:, m:i], tall_w[...])
    total += dot(left[:, i:], wide_w[m:, :])
    total += dot_nt(other[:, m:i], side[...])
    total += dot(other[:, i:], near[m:, :])
    back = total.astype(BF)
    n = mixed.shape[0] // RING
    h = n // 2
    for far0, far1, rest, value in ((*outs[:3], mixed), (*outs[3:], back)):
        far0[...] = value[2 * n : 2 * n + h, :]
        far1[...] = value[2 * n + h : 3 * n, :]
        rest[: 2 * n, :] = value[: 2 * n, :]
        rest[2 * n :, :] = value[3 * n :, :]


def products(core, left, other, tall_w, wide_w, near, side):
    rows, half = left.shape[0], near.shape[1]
    width = 512
    steps = half // width
    n = rows // RING
    whole = lambda a: pl.BlockSpec(a.shape, lambda j, c: (0, 0))
    wide = lambda a, k: pl.BlockSpec((a.shape[0], width), lambda j, c: (0, c[0] * k + j))
    tall = lambda a, k: pl.BlockSpec((width, a.shape[1]), lambda j, c: (c[0] * k + j, 0))
    counts = 2 * [n // 2, n // 2, 3 * n]
    return pl.pallas_call(
        product_kernel,
        grid_spec=pltpu.PrefetchScalarGridSpec(
            num_scalar_prefetch=1,
            grid=(steps,),
            in_specs=[
                whole(left),
                whole(other),
                tall(tall_w, steps),
                wide(wide_w, steps),
                wide(near, 0),
                tall(side, 0),
            ],
            out_specs=[pl.BlockSpec((k, width), lambda j, c: (0, j)) for k in counts],
        ),
        out_shape=[jax.ShapeDtypeStruct((k, half), BF) for k in counts],
        compiler_params=params(40),
        name="products",
    )(core, left, other, tall_w, wide_w, near, side)


def tenant_kernel(rel_tenant, values, out_bg, out_bu, out_ad):
    groups = rel_tenant.shape[0]
    some = 256
    rows = rel_tenant.shape[1]
    sub = iota((some, rows), 0)
    for out, left, first, scale in (
        (out_bg, 1, 0, 2.0),
        (out_bu, 2, RANK, 2.0),
        (out_ad, 0, 2 * RANK, 1.0),
    ):
        pick = (iota((some, LANES), 1) == (iota((some, LANES), 0) & 15) + first).astype(BF)
        sums = [jnp.zeros((some, LANES), F32) for _ in range(out.shape[0] // some)]
        for g in range(groups):
            tile = dot_nt(pick, values[g, :rows, 3 * LANES :])
            rhs = values[g, :rows, left * LANES : (left + 1) * LANES]
            who = rel_tenant[g : g + 1, :]
            for k in range(len(sums)):
                mine = (who - k * (some // RANK)) == (sub >> 4)
                sums[k] += dot(jnp.where(mine, tile, 0.0).astype(BF), rhs)
        for k, total in enumerate(sums):
            out[k * some : (k + 1) * some, :] = scale * total


def tenant_gradients(rel_tenant, values, tenants):
    shape = jax.ShapeDtypeStruct((tenants * RANK, LANES), F32)
    return pl.pallas_call(
        tenant_kernel,
        out_shape=[shape] * 3,
        compiler_params=params(40),
        name="tenant_gradients",
    )(rel_tenant, values)


def slot_kernel(weights, own, out_g, out_u, out_d):
    groups, cap = own.shape[0], own.shape[1] // 2
    x = jnp.concatenate([own[g, :cap, :] for g in range(groups)], axis=0)
    dy = jnp.concatenate([own[g, cap:, :] for g in range(groups)], axis=0)
    n = out_g.shape[0]
    both = dot(weights[: 2 * n, :], x)
    out_g[...] = both[:n, :]
    out_u[...] = both[n:, :]
    out_d[...] = dot(weights[2 * n :, :], dy)


def slot_gradients(weights, own):
    groups, rows, d = own.shape
    n = weights.shape[0] // 3
    width = 1024
    spec = pl.BlockSpec((n, width), lambda j: (0, j))
    return pl.pallas_call(
        slot_kernel,
        grid=(d // width,),
        in_specs=[
            pl.BlockSpec(weights.shape, lambda j: (0, 0)),
            pl.BlockSpec((groups, rows, width), lambda j: (0, 0, j)),
        ],
        out_specs=[spec] * 3,
        out_shape=[jax.ShapeDtypeStruct((n, d), F32)] * 3,
        compiler_params=params(32),
        name="slot_gradients",
    )(weights, own)


def add(*terms):
    total = terms[0].astype(F32)
    for t in terms[1:]:
        total = total + t.astype(F32)
    return total.astype(BF)


def first_step(a, b, axes):
    sent = []
    for p, axis in ((a, axes[0]), (b, axes[1])):
        sent += [lax.ppermute(p[0], axis, UP), lax.ppermute(p[1], axis, DOWN)]
    return lax.optimization_barrier(sent)


def second_start(a, b, axes, sent):
    moved = []
    for k, (p, axis) in enumerate(((a, axes[0]), (b, axes[1]))):
        n = p[2].shape[0] // 3
        h = n // 2
        right, left = p[2][n : 2 * n], p[2][2 * n :]
        right = jnp.concatenate([add(right[:h], sent[2 * k]), right[h:]], axis=0)
        left = jnp.concatenate([left[:h], add(left[h:], sent[2 * k + 1])], axis=0)
        moved += [lax.ppermute(right, axis, UP), lax.ppermute(left, axis, DOWN)]
    return moved


def second_end(a, b, moved, *beside):
    done = lax.optimization_barrier((*moved, *beside))
    moved, beside = done[:4], done[4:]
    own = lambda p: p[2][: p[2].shape[0] // 3]
    return add(own(a), moved[0], moved[1]), add(own(b), moved[2], moved[3]), beside


def in_pieces(v):
    n = v.shape[0] // RING
    return (
        v[2 * n : 2 * n + n // 2],
        v[2 * n + n // 2 : 3 * n],
        jnp.concatenate([v[: 2 * n], v[3 * n :]], axis=0),
    )


def local(
    tokens,
    cotangent,
    gate_weight,
    up_weight,
    down_weight,
    a_gate,
    a_up,
    down_output_factors,
    b_gate,
    b_up,
    a_down,
    tenant_of_row,
    adapter_slot,
):
    own_rows, d = tokens.shape
    half = d // CORES
    blk_count = lax.axis_size(BLK)
    grp_count = lax.axis_size("y")
    x_at, z_at, c_at, grp = (lax.axis_index(k) for k in ("x", "z", "c", "y"))
    blk = (x_at * RING + z_at) * CORES + c_at
    per_owner = a_gate.shape[0]
    tenant_count = b_gate.shape[0]
    cap = 2 * own_rows
    group_rows = own_rows * blk_count

    a_g = a_gate.reshape(per_owner * RANK, d)
    a_u = a_up.reshape(per_owner * RANK, d)
    out_f = down_output_factors.reshape(per_owner * RANK, d)
    b_g = b_gate.reshape(tenant_count * RANK, -1)
    b_u = b_up.reshape(tenant_count * RANK, -1)
    a_d = a_down.reshape(tenant_count * RANK, -1)

    all_tenants = jnp.transpose(tenant_of_row.reshape(blk_count, grp_count, own_rows), (1, 0, 2))
    all_tenants = all_tenants.reshape(grp_count, group_rows)
    hot = all_tenants[:, :, None] == jnp.arange(tenant_count, dtype=jnp.int32)
    all_slots = jnp.sum(jnp.where(hot, adapter_slot, 0), axis=2)
    all_owners = all_slots // per_owner
    at = jnp.arange(group_rows, dtype=jnp.int32)
    ahead = (all_owners[:, :, None] == all_owners[:, None, :]) & (at[:, None] > at[None, :])
    all_within = jnp.sum(ahead.astype(jnp.int32), axis=2)
    mine = all_owners == blk
    all_choose = mine[:, None, :] & (
        all_within[:, None, :] == jnp.arange(cap, dtype=jnp.int32)[None, :, None]
    )
    own_slot = jnp.sum(jnp.where(all_choose, (all_slots - per_owner * blk)[:, None, :] + 1, 0), 2) - 1
    here = lambda v: lax.dynamic_index_in_dim(v, grp, 0, keepdims=False)
    tenants, slots = here(all_tenants), here(all_slots)
    position = here(all_owners) * cap + here(all_within)
    choose = here(all_choose).astype(BF)
    rel = slots - per_owner * blk

    tall_w = jnp.concatenate([gate_weight, up_weight], axis=1)
    wide_w = jnp.concatenate([down_weight, out_f, a_g, a_u], axis=0)
    far = (1 - c_at) * half
    near = lax.ppermute(lax.dynamic_slice_in_dim(wide_w, far, half, 1), "c", SWAP)
    side = lax.ppermute(lax.dynamic_slice_in_dim(tall_w, far, half, 0), "c", SWAP)

    j = jnp.arange(group_rows, dtype=jnp.int32)
    inner = j % (CORES * own_rows)
    first, second = j // (group_rows // RING), (j // (CORES * own_rows)) % RING
    place = lambda dx, dz: (
        ((x_at + dx) % RING * RING + (z_at + dz) % RING) * CORES * own_rows + inner
    )[:, None]
    order_m, order_i = place(first, second), place(second, first)

    both = jnp.concatenate([tokens, cotangent], axis=1)
    both = lax.all_gather(both, BLK, axis=0, tiled=True)
    rel = rel[:, None]
    both, tall_w, wide_w, near, side = lax.optimization_barrier((both, tall_w, wide_w, near, side))
    pre, coef, own = project(rel, choose, both, tall_w, wide_w)
    all_own = lax.all_gather(own, "y", axis=0)
    copies = jnp.broadcast_to(coef[:, : 3 * RANK], (blk_count, cap, 3 * RANK))
    table = lax.all_to_all(copies, BLK, split_axis=0, concat_axis=0, tiled=True)
    table = jnp.pad(table.reshape(blk_count * cap, 3 * RANK), ((0, 0), (0, LANES - 3 * RANK)))
    values, placed = hidden_stage(
        tenants[:, None], position[:, None], position[None, :], table, pre, b_g, b_u, a_d
    )
    terms = placed[:, : 3 * RANK].reshape(blk_count, cap, 3 * RANK)
    terms = lax.all_to_all(terms, BLK, split_axis=0, concat_axis=0, tiled=True)
    low = jnp.sum(terms.astype(F32), axis=0).astype(BF)
    low = jnp.pad(low, ((0, cap), (0, LANES - 3 * RANK)))
    left = left_stage(rel, jnp.transpose(choose), low[:cap], order_m, order_i, values)
    other = lax.ppermute(left, "c", SWAP)
    packed = jnp.concatenate([values, low.reshape(-1, 4 * LANES)], axis=0)
    left, other, packed, all_own = lax.optimization_barrier((left, other, packed, all_own))
    packed = lax.all_gather(packed, "y", axis=0)
    pieces = products(
        c_at.reshape(1).astype(jnp.int32), left, other, tall_w, wide_w, near, side
    )
    pieces = (pieces[:3], pieces[3:])
    sent = first_step(*pieces, ("x", "z"))
    moved = second_start(*pieces, ("x", "z"), sent)
    low_all = packed[:, group_rows:, :].astype(F32)
    low_all = low_all.reshape(grp_count, -1, LANES)[:, :cap, : 3 * RANK]
    slots_dev = per_owner // grp_count
    wanted = grp * slots_dev + jnp.arange(slots_dev, dtype=jnp.int32)
    weights = jnp.where(
        (own_slot[None] == wanted[:, None, None])[:, None],
        jnp.transpose(low_all, (2, 0, 1))[None],
        0.0,
    )
    weights = weights.reshape(slots_dev, 3, RANK, grp_count * cap)
    weights = jnp.transpose(weights, (1, 0, 2, 3)).reshape(3, slots_dev * RANK, grp_count * cap)
    weights = jnp.concatenate([weights[1], weights[2], 2.0 * weights[0]], axis=0).astype(BF)
    by_slot = slot_gradients(weights, all_own)
    tenant_dev = tenant_count // grp_count
    by_tenant = tenant_gradients(all_tenants - grp * tenant_dev, packed, tenant_dev)

    *sums, grads = second_end(*pieces, moved, *by_slot, *by_tenant)
    pieces = (in_pieces(sums[0]), in_pieces(sums[1]))
    sent = first_step(*pieces, ("z", "x"))
    moved = second_start(*pieces, ("z", "x"), sent)
    *sums, _ = second_end(*pieces, moved)
    stacked = jnp.stack([v.reshape(CORES, own_rows, half) for v in sums], axis=1)
    keep = lax.dynamic_index_in_dim(stacked, c_at, 0, keepdims=False)
    give = lax.dynamic_index_in_dim(stacked, 1 - c_at, 0, keepdims=False)
    take = lax.ppermute(give, "c", SWAP)
    result = jnp.where(
        c_at == 0,
        jnp.concatenate([keep, take], axis=2),
        jnp.concatenate([take, keep], axis=2),
    )
    return (
        result[0],
        result[1],
        *(v.reshape(slots_dev, RANK, d) for v in grads[:3]),
        *(v.reshape(tenant_dev, RANK, -1) for v in grads[3:]),
    )


def solution(mesh):
    cut = Mesh(mesh.devices.reshape(RING, RING, CORES, mesh.shape["grp"]), ("x", "z", "c", "y"))
    every = (*BLK, "y")
    return jax.shard_map(
        local,
        mesh=cut,
        in_specs=(
            P(every, None),
            P(every, None),
            P(None, BLK),
            P(None, BLK),
            P(BLK, None),
            P(BLK, None, None),
            P(BLK, None, None),
            P(BLK, None, None),
            P(None, None, BLK),
            P(None, None, BLK),
            P(None, None, BLK),
            P(),
            P(),
        ),
        out_specs=(
            P(every, None),
            P(every, None),
            P(every, None, None),
            P(every, None, None),
            P(every, None, None),
            P("y", None, BLK),
            P("y", None, BLK),
            P("y", None, BLK),
        ),
        check_vma=False,
    )
```

```python
import jax
import jax.numpy as jnp
from jax import lax
from jax.experimental import pallas as pl
from jax.experimental.pallas import tpu as pltpu
from jax.sharding import Mesh
from jax.sharding import PartitionSpec as P

RING = 4
CORES = 2
BLK = ("x", "z", "c")
UP = [(i, (i + 1) % RING) for i in range(RING)]
DOWN = [(i, (i - 1) % RING) for i in range(RING)]
SWAP = [(0, 1), (1, 0)]
RANK = 16
LANES = 128
BF = jnp.bfloat16
F32 = jnp.float32


def params(mib):
    return pltpu.CompilerParams(vmem_limit_bytes=mib << 20)


def dot(a, b):
    return jnp.dot(a, b, preferred_element_type=F32)


def dot_nt(a, b):
    return lax.dot_general(a, b, (((1,), (1,)), ((), ())), preferred_element_type=F32)


def iota(shape, dim):
    return lax.broadcasted_iota(jnp.int32, shape, dim)


def folding(rows, first):
    return ((iota((rows, LANES), 0) & 15) + first == iota((rows, LANES), 1)).astype(BF)


def tiling(first, cols):
    return (iota((LANES, cols), 0) == (iota((LANES, cols), 1) & 15) + first).astype(BF)


def project_kernel(
    rel, choose, x0, x1, x2, x3, dy0, dy1, dy2, dy3, tall_w, wide_w, pre, coef, own, acc_x, acc_dy
):
    j = pl.program_id(0)

    @pl.when(j == 0)
    def _():
        acc_x[...] = jnp.zeros_like(acc_x)
        acc_dy[...] = jnp.zeros_like(acc_dy)

    xv = jnp.concatenate([r[...] for r in (x0, x1, x2, x3)], axis=0)
    dv = jnp.concatenate([r[...] for r in (dy0, dy1, dy2, dy3)], axis=0)
    acc_x[:, : 2 * LANES] += dot(xv, tall_w[...])
    acc_x[:, 2 * LANES :] += dot_nt(xv, wide_w[2 * LANES :, :])
    acc_dy[...] += dot_nt(dv, wide_w[: 2 * LANES, :])
    cap = choose.shape[0]
    own[:cap, :] = dot(choose[...], xv).astype(BF)
    own[cap:, :] = dot(choose[...], dv).astype(BF)

    @pl.when(j == pl.num_programs(0) - 1)
    def _():
        pre[:, : 2 * LANES] = acc_x[:, : 2 * LANES]
        pre[:, 2 * LANES :] = acc_dy[:, :LANES]
        rows = xv.shape[0]
        mine = rel[...] == (iota((rows, LANES), 1) >> 4)
        zero = jnp.zeros((rows, LANES), F32)
        z_g = jnp.where(mine, acc_x[:, 2 * LANES : 3 * LANES], zero).astype(BF)
        z_u = jnp.where(mine, acc_x[:, 3 * LANES :], zero).astype(BF)
        z_q = jnp.where(mine, 2.0 * acc_dy[:, LANES:], zero).astype(BF)
        packed = (
            dot(z_g, folding(LANES, 0))
            + dot(z_u, folding(LANES, RANK))
            + dot(z_q, folding(LANES, 2 * RANK))
        )
        coef[...] = dot(choose[...], packed.astype(BF)).astype(BF)


def project(rel, choose, both, tall_w, wide_w):
    rows, d = both.shape[0], both.shape[1] // 2
    cap = choose.shape[0]
    width = 1024
    steps = d // width
    return pl.pallas_call(
        project_kernel,
        grid=(steps,),
        in_specs=[
            pl.BlockSpec((rows, 1), lambda j: (0, 0)),
            pl.BlockSpec((cap, rows), lambda j: (0, 0)),
            *(pl.BlockSpec((rows // 4, width), lambda j, k=k: (k, j)) for k in range(4)),
            *(pl.BlockSpec((rows // 4, width), lambda j, k=k: (k, j + steps)) for k in range(4)),
            pl.BlockSpec((width, tall_w.shape[1]), lambda j: (j, 0)),
            pl.BlockSpec((wide_w.shape[0], width), lambda j: (0, j)),
        ],
        out_specs=[
            pl.BlockSpec((rows, 3 * LANES), lambda j: (0, 0)),
            pl.BlockSpec((cap, LANES), lambda j: (0, 0)),
            pl.BlockSpec((2 * cap, width), lambda j: (0, j)),
        ],
        out_shape=[
            jax.ShapeDtypeStruct((rows, 3 * LANES), F32),
            jax.ShapeDtypeStruct((cap, LANES), BF),
            jax.ShapeDtypeStruct((2 * cap, d), BF),
        ],
        scratch_shapes=[pltpu.VMEM((rows, 4 * LANES), F32), pltpu.VMEM((rows, 2 * LANES), F32)],
        compiler_params=params(56),
        name="project",
    )(rel, choose, *([both] * 8), tall_w, wide_w)


def hidden_kernel(tenant, pos, pos_row, table, pre, b_g, b_u, a_d, values, placed, partial):
    j = pl.program_id(0)
    rows = pre.shape[0]
    wide = 512
    spots = table.shape[0]
    here = (pos[...] == iota((rows, spots), 1)).astype(BF)
    coefs = dot(here, table[...]).astype(BF)
    tiles = [dot(coefs, tiling(k * RANK, wide)) for k in range(3)]
    who = tenant[...]
    extra = [jnp.zeros((rows, LANES), F32) for _ in range(3)]
    factors = (b_g, b_u, a_d)
    count = b_g.shape[0] // wide
    lane_tenant = iota((rows, wide), 1) >> 4
    for k in range(count):
        mine = (who - k * (wide // RANK)) == lane_tenant
        for m in range(3):
            e = jnp.where(mine, tiles[m], 0.0).astype(BF)
            extra[m] += dot(e, factors[m][k * wide : (k + 1) * wide, :])
    gate = pre[:, :LANES] + 2.0 * extra[0]
    up = pre[:, LANES : 2 * LANES] + 2.0 * extra[1]
    grad = pre[:, 2 * LANES :] + extra[2]
    sig = 1.0 / (1.0 + jnp.exp(-gate))
    act = gate * sig
    slope = sig * (1.0 + gate * (1.0 - sig))
    hidden = (act * up).astype(BF)
    grad_gate = (grad * up * slope).astype(BF)
    grad_up = (grad * act).astype(BF)
    values[:, :LANES] = hidden
    values[:, LANES : 2 * LANES] = grad_gate
    values[:, 2 * LANES : 3 * LANES] = grad_up
    values[:, 3 * LANES :] = coefs
    low = jnp.zeros((rows, LANES), F32)
    for left, right, first, scale in (
        (hidden, a_d, 0, 1.0),
        (grad_gate, b_g, RANK, 2.0),
        (grad_up, b_u, 2 * RANK, 2.0),
    ):
        total = jnp.zeros((rows, wide), F32)
        for k in range(count):
            mine = (who - k * (wide // RANK)) == lane_tenant
            z = dot_nt(left, right[k * wide : (k + 1) * wide, :])
            total = jnp.where(mine, z, total)
        low += dot((scale * total).astype(BF), folding(wide, first))
    partial[pl.ds(pl.multiple_of(j * rows, rows), rows), :] = low.astype(BF)

    @pl.when(j == pl.num_programs(0) - 1)
    def _():
        every = partial.shape[0]
        put = (pos_row[...] == iota((spots, every), 0)).astype(BF)
        placed[...] = dot(put, partial[...]).astype(BF)


def hidden_stage(tenant, pos, pos_row, table, pre, b_g, b_u, a_d):
    rows = pre.shape[0]
    part = 256
    whole = lambda a: pl.BlockSpec(a.shape, lambda j: (0, 0))
    spots = table.shape[0]
    return pl.pallas_call(
        hidden_kernel,
        grid=(rows // part,),
        in_specs=[
            pl.BlockSpec((part, 1), lambda j: (j, 0)),
            pl.BlockSpec((part, 1), lambda j: (j, 0)),
            whole(pos_row),
            whole(table),
            pl.BlockSpec((part, 3 * LANES), lambda j: (j, 0)),
            whole(b_g),
            whole(b_u),
            whole(a_d),
        ],
        out_specs=[
            pl.BlockSpec((part, 4 * LANES), lambda j: (j, 0)),
            pl.BlockSpec((spots, LANES), lambda j: (0, 0)),
        ],
        out_shape=[
            jax.ShapeDtypeStruct((rows, 4 * LANES), BF),
            jax.ShapeDtypeStruct((spots, LANES), BF),
        ],
        scratch_shapes=[pltpu.VMEM((rows, LANES), BF)],
        compiler_params=params(56),
        name="hidden_stage",
    )(tenant, pos, pos_row, table, pre, b_g, b_u, a_d)


def left_kernel(rel, choose_t, low, order_m, order_i, values, left, packed):
    rows = rel.shape[0]
    mine = rel[...] == (iota((rows, LANES), 1) >> 4)
    back = dot(choose_t[...], low[...]).astype(BF)
    spread = lambda first, scale: jnp.where(
        mine, scale * dot(back, tiling(first, LANES)), 0.0
    ).astype(BF)
    for_mixed = jnp.concatenate([values[:, :LANES], spread(0, 2.0)], axis=1)
    for_input = jnp.concatenate(
        [values[:, LANES : 3 * LANES], spread(RANK, 1.0), spread(2 * RANK, 1.0)], axis=1
    )
    packed[:rows, :] = values[...]
    packed[rows:, :] = jnp.zeros((packed.shape[0] - rows, packed.shape[1]), BF)
    packed[rows:, :LANES] = low[...]
    at = iota((rows, rows), 1)
    left[:, : 2 * LANES] = dot((order_m[...] == at).astype(BF), for_mixed).astype(BF)
    left[:, 2 * LANES :] = dot((order_i[...] == at).astype(BF), for_input).astype(BF)


def left_stage(rel, choose_t, low, order_m, order_i, values):
    rows = rel.shape[0]
    return pl.pallas_call(
        left_kernel,
        out_shape=[
            jax.ShapeDtypeStruct((rows, 6 * LANES), BF),
            jax.ShapeDtypeStruct((rows + low.shape[0], values.shape[1]), BF),
        ],
        compiler_params=params(56),
        name="left_stage",
    )(rel, choose_t, low, order_m, order_i, values)


def product_kernel(core, left, other, tall_w, wide_w, near, side, *outs):
    del core
    m, i = 2 * LANES, 4 * LANES
    total = dot(left[:, :m], wide_w[:m, :])
    total += dot(other[:, :m], near[:m, :])
    mixed = total.astype(BF)
    total = dot_nt(left[:, m:i], tall_w[...])
    total += dot(left[:, i:], wide_w[m:, :])
    total += dot_nt(other[:, m:i], side[...])
    total += dot(other[:, i:], near[m:, :])
    back = total.astype(BF)
    n = mixed.shape[0] // RING
    h = n // 2
    for far0, far1, rest, value in ((*outs[:3], mixed), (*outs[3:], back)):
        far0[...] = value[2 * n : 2 * n + h, :]
        far1[...] = value[2 * n + h : 3 * n, :]
        rest[: 2 * n, :] = value[: 2 * n, :]
        rest[2 * n :, :] = value[3 * n :, :]


def products(core, left, other, tall_w, wide_w, near, side):
    rows, half = left.shape[0], near.shape[1]
    width = 512
    steps = half // width
    n = rows // RING
    whole = lambda a: pl.BlockSpec(a.shape, lambda j, c: (0, 0))
    wide = lambda a, k: pl.BlockSpec((a.shape[0], width), lambda j, c: (0, c[0] * k + j))
    tall = lambda a, k: pl.BlockSpec((width, a.shape[1]), lambda j, c: (c[0] * k + j, 0))
    counts = 2 * [n // 2, n // 2, 3 * n]
    return pl.pallas_call(
        product_kernel,
        grid_spec=pltpu.PrefetchScalarGridSpec(
            num_scalar_prefetch=1,
            grid=(steps,),
            in_specs=[
                whole(left),
                whole(other),
                tall(tall_w, steps),
                wide(wide_w, steps),
                wide(near, 0),
                tall(side, 0),
            ],
            out_specs=[pl.BlockSpec((k, width), lambda j, c: (0, j)) for k in counts],
        ),
        out_shape=[jax.ShapeDtypeStruct((k, half), BF) for k in counts],
        compiler_params=params(56),
        name="products",
    )(core, left, other, tall_w, wide_w, near, side)


def tenant_kernel(rel_tenant, values, out_bg, out_bu, out_ad):
    groups = rel_tenant.shape[0]
    some = 256
    rows = rel_tenant.shape[1]
    sub = iota((some, rows), 0)
    for out, left, first, scale in (
        (out_bg, 1, 0, 2.0),
        (out_bu, 2, RANK, 2.0),
        (out_ad, 0, 2 * RANK, 1.0),
    ):
        pick = (iota((some, LANES), 1) == (iota((some, LANES), 0) & 15) + first).astype(BF)
        sums = [jnp.zeros((some, LANES), F32) for _ in range(out.shape[0] // some)]
        for g in range(groups):
            tile = dot_nt(pick, values[g, :rows, 3 * LANES :])
            rhs = values[g, :rows, left * LANES : (left + 1) * LANES]
            who = rel_tenant[g : g + 1, :]
            for k in range(len(sums)):
                mine = (who - k * (some // RANK)) == (sub >> 4)
                sums[k] += dot(jnp.where(mine, tile, 0.0).astype(BF), rhs)
        for k, total in enumerate(sums):
            out[k * some : (k + 1) * some, :] = scale * total


def tenant_gradients(rel_tenant, values, tenants):
    shape = jax.ShapeDtypeStruct((tenants * RANK, LANES), F32)
    return pl.pallas_call(
        tenant_kernel,
        out_shape=[shape] * 3,
        compiler_params=params(56),
        name="tenant_gradients",
    )(rel_tenant, values)


def slot_kernel(weights, own, out_g, out_u, out_d):
    groups, cap = own.shape[0], own.shape[1] // 2
    x = jnp.concatenate([own[g, :cap, :] for g in range(groups)], axis=0)
    dy = jnp.concatenate([own[g, cap:, :] for g in range(groups)], axis=0)
    n = out_g.shape[0]
    both = dot(weights[: 2 * n, :], x)
    out_g[...] = both[:n, :]
    out_u[...] = both[n:, :]
    out_d[...] = dot(weights[2 * n :, :], dy)


def slot_gradients(weights, own):
    groups, rows, d = own.shape
    n = weights.shape[0] // 3
    width = 1024
    spec = pl.BlockSpec((n, width), lambda j: (0, j))
    return pl.pallas_call(
        slot_kernel,
        grid=(d // width,),
        in_specs=[
            pl.BlockSpec(weights.shape, lambda j: (0, 0)),
            pl.BlockSpec((groups, rows, width), lambda j: (0, 0, j)),
        ],
        out_specs=[spec] * 3,
        out_shape=[jax.ShapeDtypeStruct((n, d), F32)] * 3,
        compiler_params=params(56),
        name="slot_gradients",
    )(weights, own)


def add(*terms):
    total = terms[0].astype(F32)
    for t in terms[1:]:
        total = total + t.astype(F32)
    return total.astype(BF)


def first_step(a, b, axes):
    sent = []
    for p, axis in ((a, axes[0]), (b, axes[1])):
        sent += [lax.ppermute(p[0], axis, UP), lax.ppermute(p[1], axis, DOWN)]
    return lax.optimization_barrier(sent)


def second_start(a, b, axes, sent):
    moved = []
    for k, (p, axis) in enumerate(((a, axes[0]), (b, axes[1]))):
        n = p[2].shape[0] // 3
        h = n // 2
        right, left = p[2][n : 2 * n], p[2][2 * n :]
        right = jnp.concatenate([add(right[:h], sent[2 * k]), right[h:]], axis=0)
        left = jnp.concatenate([left[:h], add(left[h:], sent[2 * k + 1])], axis=0)
        moved += [lax.ppermute(right, axis, UP), lax.ppermute(left, axis, DOWN)]
    return moved


def second_end(a, b, moved, *beside):
    done = lax.optimization_barrier((*moved, *beside))
    moved, beside = done[:4], done[4:]
    own = lambda p: p[2][: p[2].shape[0] // 3]
    return add(own(a), moved[0], moved[1]), add(own(b), moved[2], moved[3]), beside


def in_pieces(v):
    n = v.shape[0] // RING
    return (
        v[2 * n : 2 * n + n // 2],
        v[2 * n + n // 2 : 3 * n],
        jnp.concatenate([v[: 2 * n], v[3 * n :]], axis=0),
    )


def local(
    tokens,
    cotangent,
    gate_weight,
    up_weight,
    down_weight,
    a_gate,
    a_up,
    down_output_factors,
    b_gate,
    b_up,
    a_down,
    tenant_of_row,
    adapter_slot,
):
    own_rows, d = tokens.shape
    half = d // CORES
    blk_count = lax.axis_size(BLK)
    grp_count = lax.axis_size("y")
    x_at, z_at, c_at, grp = (lax.axis_index(k) for k in ("x", "z", "c", "y"))
    blk = (x_at * RING + z_at) * CORES + c_at
    per_owner = a_gate.shape[0]
    tenant_count = b_gate.shape[0]
    cap = 2 * own_rows
    group_rows = own_rows * blk_count

    a_g = a_gate.reshape(per_owner * RANK, d)
    a_u = a_up.reshape(per_owner * RANK, d)
    out_f = down_output_factors.reshape(per_owner * RANK, d)
    b_g = b_gate.reshape(tenant_count * RANK, -1)
    b_u = b_up.reshape(tenant_count * RANK, -1)
    a_d = a_down.reshape(tenant_count * RANK, -1)

    all_tenants = jnp.transpose(tenant_of_row.reshape(blk_count, grp_count, own_rows), (1, 0, 2))
    all_tenants = all_tenants.reshape(grp_count, group_rows)
    hot = all_tenants[:, :, None] == jnp.arange(tenant_count, dtype=jnp.int32)
    all_slots = jnp.sum(jnp.where(hot, adapter_slot, 0), axis=2)
    all_owners = all_slots // per_owner
    at = jnp.arange(group_rows, dtype=jnp.int32)
    ahead = (all_owners[:, :, None] == all_owners[:, None, :]) & (at[:, None] > at[None, :])
    all_within = jnp.sum(ahead.astype(jnp.int32), axis=2)
    mine = all_owners == blk
    all_choose = mine[:, None, :] & (
        all_within[:, None, :] == jnp.arange(cap, dtype=jnp.int32)[None, :, None]
    )
    own_slot = jnp.sum(jnp.where(all_choose, (all_slots - per_owner * blk)[:, None, :] + 1, 0), 2) - 1
    here = lambda v: lax.dynamic_index_in_dim(v, grp, 0, keepdims=False)
    tenants, slots = here(all_tenants), here(all_slots)
    position = here(all_owners) * cap + here(all_within)
    choose = here(all_choose).astype(BF)
    rel = slots - per_owner * blk

    tall_w = jnp.concatenate([gate_weight, up_weight], axis=1)
    wide_w = jnp.concatenate([down_weight, out_f, a_g, a_u], axis=0)
    far = (1 - c_at) * half
    near = lax.ppermute(lax.dynamic_slice_in_dim(wide_w, far, half, 1), "c", SWAP)
    side = lax.ppermute(lax.dynamic_slice_in_dim(tall_w, far, half, 0), "c", SWAP)

    j = jnp.arange(group_rows, dtype=jnp.int32)
    inner = j % (CORES * own_rows)
    first, second = j // (group_rows // RING), (j // (CORES * own_rows)) % RING
    place = lambda dx, dz: (
        ((x_at + dx) % RING * RING + (z_at + dz) % RING) * CORES * own_rows + inner
    )[:, None]
    order_m, order_i = place(first, second), place(second, first)

    both = jnp.concatenate([tokens, cotangent], axis=1)
    both = lax.all_gather(both, BLK, axis=0, tiled=True)
    rel = rel[:, None]
    both, tall_w, wide_w, near, side = lax.optimization_barrier((both, tall_w, wide_w, near, side))
    pre, coef, own = project(rel, choose, both, tall_w, wide_w)
    all_own = lax.all_gather(own, "y", axis=0)
    copies = jnp.broadcast_to(coef[:, : 3 * RANK], (blk_count, cap, 3 * RANK))
    table = lax.all_to_all(copies, BLK, split_axis=0, concat_axis=0, tiled=True)
    table = jnp.pad(table.reshape(blk_count * cap, 3 * RANK), ((0, 0), (0, LANES - 3 * RANK)))
    values, placed = hidden_stage(
        tenants[:, None], position[:, None], position[None, :], table, pre, b_g, b_u, a_d
    )
    terms = placed[:, : 3 * RANK].reshape(blk_count, cap, 3 * RANK)
    terms = lax.all_to_all(terms, BLK, split_axis=0, concat_axis=0, tiled=True)
    low = jnp.sum(terms.astype(F32), axis=0).astype(BF)
    low = jnp.pad(low, ((0, 0), (0, LANES - 3 * RANK)))
    left, packed = left_stage(rel, jnp.transpose(choose), low, order_m, order_i, values)
    other = lax.ppermute(left, "c", SWAP)
    left, other, packed, all_own = lax.optimization_barrier((left, other, packed, all_own))
    packed = lax.all_gather(packed, "y", axis=0)
    pieces = products(
        c_at.reshape(1).astype(jnp.int32), left, other, tall_w, wide_w, near, side
    )
    pieces = (pieces[:3], pieces[3:])
    sent = first_step(*pieces, ("x", "z"))
    moved = second_start(*pieces, ("x", "z"), sent)
    low_all = packed[:, group_rows:, : 3 * RANK].astype(F32)
    slots_dev = per_owner // grp_count
    wanted = grp * slots_dev + jnp.arange(slots_dev, dtype=jnp.int32)
    weights = jnp.where(
        (own_slot[None] == wanted[:, None, None])[:, None],
        jnp.transpose(low_all, (2, 0, 1))[None],
        0.0,
    )
    weights = weights.reshape(slots_dev, 3, RANK, grp_count * cap)
    weights = jnp.transpose(weights, (1, 0, 2, 3)).reshape(3, slots_dev * RANK, grp_count * cap)
    weights = jnp.concatenate([weights[1], weights[2], 2.0 * weights[0]], axis=0).astype(BF)
    by_slot = slot_gradients(weights, all_own)
    tenant_dev = tenant_count // grp_count
    by_tenant = tenant_gradients(all_tenants - grp * tenant_dev, packed, tenant_dev)

    *sums, grads = second_end(*pieces, moved, *by_slot, *by_tenant)
    pieces = (in_pieces(sums[0]), in_pieces(sums[1]))
    sent = first_step(*pieces, ("z", "x"))
    moved = second_start(*pieces, ("z", "x"), sent)
    *sums, _ = second_end(*pieces, moved)
    stacked = jnp.stack([v.reshape(CORES, own_rows, half) for v in sums], axis=1)
    keep = lax.dynamic_index_in_dim(stacked, c_at, 0, keepdims=False)
    give = lax.dynamic_index_in_dim(stacked, 1 - c_at, 0, keepdims=False)
    take = lax.ppermute(give, "c", SWAP)
    result = jnp.where(
        c_at == 0,
        jnp.concatenate([keep, take], axis=2),
        jnp.concatenate([take, keep], axis=2),
    )
    return (
        result[0],
        result[1],
        *(v.reshape(slots_dev, RANK, d) for v in grads[:3]),
        *(v.reshape(tenant_dev, RANK, -1) for v in grads[3:]),
    )


def solution(mesh):
    cut = Mesh(mesh.devices.reshape(RING, RING, CORES, mesh.shape["grp"]), ("x", "z", "c", "y"))
    every = (*BLK, "y")
    return jax.shard_map(
        local,
        mesh=cut,
        in_specs=(
            P(every, None),
            P(every, None),
            P(None, BLK),
            P(None, BLK),
            P(BLK, None),
            P(BLK, None, None),
            P(BLK, None, None),
            P(BLK, None, None),
            P(None, None, BLK),
            P(None, None, BLK),
            P(None, None, BLK),
            P(),
            P(),
        ),
        out_specs=(
            P(every, None),
            P(every, None),
            P(every, None, None),
            P(every, None, None),
            P(every, None, None),
            P("y", None, BLK),
            P("y", None, BLK),
            P("y", None, BLK),
        ),
        check_vma=False,
    )
```

```python
import jax
import jax.numpy as jnp
from jax import lax
from jax.experimental import pallas as pl
from jax.experimental.pallas import tpu as pltpu
from jax.sharding import Mesh
from jax.sharding import PartitionSpec as P

RING = 4
CORES = 2
BLK = ("x", "z", "c")
UP = [(i, (i + 1) % RING) for i in range(RING)]
DOWN = [(i, (i - 1) % RING) for i in range(RING)]
SWAP = [(0, 1), (1, 0)]
RANK = 16
LANES = 128
BF = jnp.bfloat16
F32 = jnp.float32


def params(mib):
    return pltpu.CompilerParams(vmem_limit_bytes=mib << 20)


def dot(a, b):
    return jnp.dot(a, b, preferred_element_type=F32)


def dot_nt(a, b):
    return lax.dot_general(a, b, (((1,), (1,)), ((), ())), preferred_element_type=F32)


def iota(shape, dim):
    return lax.broadcasted_iota(jnp.int32, shape, dim)


def folding(rows, first):
    return ((iota((rows, LANES), 0) & 15) + first == iota((rows, LANES), 1)).astype(BF)


def tiling(first, cols):
    return (iota((LANES, cols), 0) == (iota((LANES, cols), 1) & 15) + first).astype(BF)


def project_kernel(
    rel, choose, x0, x1, x2, x3, dy0, dy1, dy2, dy3, tall_w, wide_w, pre, coef, own, acc_x, acc_dy
):
    j = pl.program_id(0)

    @pl.when(j == 0)
    def _():
        acc_x[...] = jnp.zeros_like(acc_x)
        acc_dy[...] = jnp.zeros_like(acc_dy)

    xv = jnp.concatenate([r[...] for r in (x0, x1, x2, x3)], axis=0)
    dv = jnp.concatenate([r[...] for r in (dy0, dy1, dy2, dy3)], axis=0)
    acc_x[:, : 2 * LANES] += dot(xv, tall_w[...])
    acc_x[:, 2 * LANES :] += dot_nt(xv, wide_w[2 * LANES :, :])
    acc_dy[...] += dot_nt(dv, wide_w[: 2 * LANES, :])
    cap = choose.shape[0]
    own[:cap, :] = dot(choose[...], xv).astype(BF)
    own[cap:, :] = dot(choose[...], dv).astype(BF)

    @pl.when(j == pl.num_programs(0) - 1)
    def _():
        pre[:, : 2 * LANES] = acc_x[:, : 2 * LANES]
        pre[:, 2 * LANES :] = acc_dy[:, :LANES]
        rows = xv.shape[0]
        mine = rel[...] == (iota((rows, LANES), 1) >> 4)
        zero = jnp.zeros((rows, LANES), F32)
        z_g = jnp.where(mine, acc_x[:, 2 * LANES : 3 * LANES], zero).astype(BF)
        z_u = jnp.where(mine, acc_x[:, 3 * LANES :], zero).astype(BF)
        z_q = jnp.where(mine, 2.0 * acc_dy[:, LANES:], zero).astype(BF)
        packed = (
            dot(z_g, folding(LANES, 0))
            + dot(z_u, folding(LANES, RANK))
            + dot(z_q, folding(LANES, 2 * RANK))
        )
        coef[...] = dot(choose[...], packed.astype(BF)).astype(BF)


def project(rel, choose, both, tall_w, wide_w):
    rows, d = both.shape[0], both.shape[1] // 2
    cap = choose.shape[0]
    width = 2048
    steps = d // width
    return pl.pallas_call(
        project_kernel,
        grid=(steps,),
        in_specs=[
            pl.BlockSpec((rows, 1), lambda j: (0, 0)),
            pl.BlockSpec((cap, rows), lambda j: (0, 0)),
            *(pl.BlockSpec((rows // 4, width), lambda j, k=k: (k, j)) for k in range(4)),
            *(pl.BlockSpec((rows // 4, width), lambda j, k=k: (k, j + steps)) for k in range(4)),
            pl.BlockSpec((width, tall_w.shape[1]), lambda j: (j, 0)),
            pl.BlockSpec((wide_w.shape[0], width), lambda j: (0, j)),
        ],
        out_specs=[
            pl.BlockSpec((rows, 3 * LANES), lambda j: (0, 0)),
            pl.BlockSpec((cap, LANES), lambda j: (0, 0)),
            pl.BlockSpec((2 * cap, width), lambda j: (0, j)),
        ],
        out_shape=[
            jax.ShapeDtypeStruct((rows, 3 * LANES), F32),
            jax.ShapeDtypeStruct((cap, LANES), BF),
            jax.ShapeDtypeStruct((2 * cap, d), BF),
        ],
        scratch_shapes=[pltpu.VMEM((rows, 4 * LANES), F32), pltpu.VMEM((rows, 2 * LANES), F32)],
        compiler_params=params(56),
        name="project",
    )(rel, choose, *([both] * 8), tall_w, wide_w)


def hidden_kernel(tenant, pos, pos_row, table, pre, b_g, b_u, a_d, values, placed, partial):
    j = pl.program_id(0)
    rows = pre.shape[0]
    wide = 512
    spots = table.shape[0]
    here = (pos[...] == iota((rows, spots), 1)).astype(BF)
    coefs = dot(here, table[...]).astype(BF)
    tiles = [dot(coefs, tiling(k * RANK, wide)) for k in range(3)]
    who = tenant[...]
    extra = [jnp.zeros((rows, LANES), F32) for _ in range(3)]
    factors = (b_g, b_u, a_d)
    count = b_g.shape[0] // wide
    lane_tenant = iota((rows, wide), 1) >> 4
    for k in range(count):
        mine = (who - k * (wide // RANK)) == lane_tenant
        for m in range(3):
            e = jnp.where(mine, tiles[m], 0.0).astype(BF)
            extra[m] += dot(e, factors[m][k * wide : (k + 1) * wide, :])
    gate = pre[:, :LANES] + 2.0 * extra[0]
    up = pre[:, LANES : 2 * LANES] + 2.0 * extra[1]
    grad = pre[:, 2 * LANES :] + extra[2]
    sig = 1.0 / (1.0 + jnp.exp(-gate))
    act = gate * sig
    slope = sig * (1.0 + gate * (1.0 - sig))
    hidden = (act * up).astype(BF)
    grad_gate = (grad * up * slope).astype(BF)
    grad_up = (grad * act).astype(BF)
    values[:, :LANES] = hidden
    values[:, LANES : 2 * LANES] = grad_gate
    values[:, 2 * LANES : 3 * LANES] = grad_up
    values[:, 3 * LANES :] = coefs
    low = jnp.zeros((rows, LANES), F32)
    for left, right, first, scale in (
        (hidden, a_d, 0, 1.0),
        (grad_gate, b_g, RANK, 2.0),
        (grad_up, b_u, 2 * RANK, 2.0),
    ):
        total = jnp.zeros((rows, wide), F32)
        for k in range(count):
            mine = (who - k * (wide // RANK)) == lane_tenant
            z = dot_nt(left, right[k * wide : (k + 1) * wide, :])
            total = jnp.where(mine, z, total)
        low += dot((scale * total).astype(BF), folding(wide, first))
    partial[pl.ds(pl.multiple_of(j * rows, rows), rows), :] = low.astype(BF)

    @pl.when(j == pl.num_programs(0) - 1)
    def _():
        every = partial.shape[0]
        put = (pos_row[...] == iota((spots, every), 0)).astype(BF)
        placed[...] = dot(put, partial[...]).astype(BF)


def hidden_stage(tenant, pos, pos_row, table, pre, b_g, b_u, a_d):
    rows = pre.shape[0]
    part = 512
    whole = lambda a: pl.BlockSpec(a.shape, lambda j: (0, 0))
    spots = table.shape[0]
    return pl.pallas_call(
        hidden_kernel,
        grid=(rows // part,),
        in_specs=[
            pl.BlockSpec((part, 1), lambda j: (j, 0)),
            pl.BlockSpec((part, 1), lambda j: (j, 0)),
            whole(pos_row),
            whole(table),
            pl.BlockSpec((part, 3 * LANES), lambda j: (j, 0)),
            whole(b_g),
            whole(b_u),
            whole(a_d),
        ],
        out_specs=[
            pl.BlockSpec((part, 4 * LANES), lambda j: (j, 0)),
            pl.BlockSpec((spots, LANES), lambda j: (0, 0)),
        ],
        out_shape=[
            jax.ShapeDtypeStruct((rows, 4 * LANES), BF),
            jax.ShapeDtypeStruct((spots, LANES), BF),
        ],
        scratch_shapes=[pltpu.VMEM((rows, LANES), BF)],
        compiler_params=params(56),
        name="hidden_stage",
    )(tenant, pos, pos_row, table, pre, b_g, b_u, a_d)


def left_kernel(rel, choose_t, low, order_m, order_i, values, left, packed):
    rows = rel.shape[0]
    mine = rel[...] == (iota((rows, LANES), 1) >> 4)
    back = dot(choose_t[...], low[...]).astype(BF)
    spread = lambda first, scale: jnp.where(
        mine, scale * dot(back, tiling(first, LANES)), 0.0
    ).astype(BF)
    for_mixed = jnp.concatenate([values[:, :LANES], spread(0, 2.0)], axis=1)
    for_input = jnp.concatenate(
        [values[:, LANES : 3 * LANES], spread(RANK, 1.0), spread(2 * RANK, 1.0)], axis=1
    )
    packed[:rows, :] = values[...]
    packed[rows:, :] = jnp.zeros((packed.shape[0] - rows, packed.shape[1]), BF)
    packed[rows:, :LANES] = low[...]
    at = iota((rows, rows), 1)
    left[:, : 2 * LANES] = dot((order_m[...] == at).astype(BF), for_mixed).astype(BF)
    left[:, 2 * LANES :] = dot((order_i[...] == at).astype(BF), for_input).astype(BF)


def left_stage(rel, choose_t, low, order_m, order_i, values):
    rows = rel.shape[0]
    return pl.pallas_call(
        left_kernel,
        out_shape=[
            jax.ShapeDtypeStruct((rows, 6 * LANES), BF),
            jax.ShapeDtypeStruct((rows + low.shape[0], values.shape[1]), BF),
        ],
        compiler_params=params(56),
        name="left_stage",
    )(rel, choose_t, low, order_m, order_i, values)


def product_kernel(core, left, other, tall_w, wide_w, near, side, *outs):
    del core
    m, i = 2 * LANES, 4 * LANES
    total = dot(left[:, :m], wide_w[:m, :])
    total += dot(other[:, :m], near[:m, :])
    mixed = total.astype(BF)
    total = dot_nt(left[:, m:i], tall_w[...])
    total += dot(left[:, i:], wide_w[m:, :])
    total += dot_nt(other[:, m:i], side[...])
    total += dot(other[:, i:], near[m:, :])
    back = total.astype(BF)
    n = mixed.shape[0] // RING
    h = n // 2
    for far0, far1, rest, value in ((*outs[:3], mixed), (*outs[3:], back)):
        far0[...] = value[2 * n : 2 * n + h, :]
        far1[...] = value[2 * n + h : 3 * n, :]
        rest[: 2 * n, :] = value[: 2 * n, :]
        rest[2 * n :, :] = value[3 * n :, :]


def products(core, left, other, tall_w, wide_w, near, side):
    rows, half = left.shape[0], near.shape[1]
    width = 512
    steps = half // width
    n = rows // RING
    whole = lambda a: pl.BlockSpec(a.shape, lambda j, c: (0, 0))
    wide = lambda a, k: pl.BlockSpec((a.shape[0], width), lambda j, c: (0, c[0] * k + j))
    tall = lambda a, k: pl.BlockSpec((width, a.shape[1]), lambda j, c: (c[0] * k + j, 0))
    counts = 2 * [n // 2, n // 2, 3 * n]
    return pl.pallas_call(
        product_kernel,
        grid_spec=pltpu.PrefetchScalarGridSpec(
            num_scalar_prefetch=1,
            grid=(steps,),
            in_specs=[
                whole(left),
                whole(other),
                tall(tall_w, steps),
                wide(wide_w, steps),
                wide(near, 0),
                tall(side, 0),
            ],
            out_specs=[pl.BlockSpec((k, width), lambda j, c: (0, j)) for k in counts],
        ),
        out_shape=[jax.ShapeDtypeStruct((k, half), BF) for k in counts],
        compiler_params=params(56),
        name="products",
    )(core, left, other, tall_w, wide_w, near, side)


def tenant_kernel(rel_tenant, values, out_bg, out_bu, out_ad):
    groups = rel_tenant.shape[0]
    some = 256
    rows = rel_tenant.shape[1]
    sub = iota((some, rows), 0)
    for out, left, first, scale in (
        (out_bg, 1, 0, 2.0),
        (out_bu, 2, RANK, 2.0),
        (out_ad, 0, 2 * RANK, 1.0),
    ):
        pick = (iota((some, LANES), 1) == (iota((some, LANES), 0) & 15) + first).astype(BF)
        sums = [jnp.zeros((some, LANES), F32) for _ in range(out.shape[0] // some)]
        for g in range(groups):
            tile = dot_nt(pick, values[g, :rows, 3 * LANES :])
            rhs = values[g, :rows, left * LANES : (left + 1) * LANES]
            who = rel_tenant[g : g + 1, :]
            for k in range(len(sums)):
                mine = (who - k * (some // RANK)) == (sub >> 4)
                sums[k] += dot(jnp.where(mine, tile, 0.0).astype(BF), rhs)
        for k, total in enumerate(sums):
            out[k * some : (k + 1) * some, :] = scale * total


def tenant_gradients(rel_tenant, values, tenants):
    shape = jax.ShapeDtypeStruct((tenants * RANK, LANES), F32)
    return pl.pallas_call(
        tenant_kernel,
        out_shape=[shape] * 3,
        compiler_params=params(56),
        name="tenant_gradients",
    )(rel_tenant, values)


def slot_kernel(weights, own, out_g, out_u, out_d):
    groups, cap = own.shape[0], own.shape[1] // 2
    x = jnp.concatenate([own[g, :cap, :] for g in range(groups)], axis=0)
    dy = jnp.concatenate([own[g, cap:, :] for g in range(groups)], axis=0)
    n = out_g.shape[0]
    both = dot(weights[: 2 * n, :], x)
    out_g[...] = both[:n, :]
    out_u[...] = both[n:, :]
    out_d[...] = dot(weights[2 * n :, :], dy)


def slot_gradients(weights, own):
    groups, rows, d = own.shape
    n = weights.shape[0] // 3
    width = 1024
    spec = pl.BlockSpec((n, width), lambda j: (0, j))
    return pl.pallas_call(
        slot_kernel,
        grid=(d // width,),
        in_specs=[
            pl.BlockSpec(weights.shape, lambda j: (0, 0)),
            pl.BlockSpec((groups, rows, width), lambda j: (0, 0, j)),
        ],
        out_specs=[spec] * 3,
        out_shape=[jax.ShapeDtypeStruct((n, d), F32)] * 3,
        compiler_params=params(56),
        name="slot_gradients",
    )(weights, own)


def add(*terms):
    total = terms[0].astype(F32)
    for t in terms[1:]:
        total = total + t.astype(F32)
    return total.astype(BF)


def first_step(a, b, axes):
    sent = []
    for p, axis in ((a, axes[0]), (b, axes[1])):
        sent += [lax.ppermute(p[0], axis, UP), lax.ppermute(p[1], axis, DOWN)]
    return lax.optimization_barrier(sent)


def second_start(a, b, axes, sent):
    moved = []
    for k, (p, axis) in enumerate(((a, axes[0]), (b, axes[1]))):
        n = p[2].shape[0] // 3
        h = n // 2
        right, left = p[2][n : 2 * n], p[2][2 * n :]
        right = jnp.concatenate([add(right[:h], sent[2 * k]), right[h:]], axis=0)
        left = jnp.concatenate([left[:h], add(left[h:], sent[2 * k + 1])], axis=0)
        moved += [lax.ppermute(right, axis, UP), lax.ppermute(left, axis, DOWN)]
    return moved


def second_end(a, b, moved, *beside):
    done = lax.optimization_barrier((*moved, *beside))
    moved, beside = done[:4], done[4:]
    own = lambda p: p[2][: p[2].shape[0] // 3]
    return add(own(a), moved[0], moved[1]), add(own(b), moved[2], moved[3]), beside


def in_pieces(v):
    n = v.shape[0] // RING
    return (
        v[2 * n : 2 * n + n // 2],
        v[2 * n + n // 2 : 3 * n],
        jnp.concatenate([v[: 2 * n], v[3 * n :]], axis=0),
    )


def local(
    tokens,
    cotangent,
    gate_weight,
    up_weight,
    down_weight,
    a_gate,
    a_up,
    down_output_factors,
    b_gate,
    b_up,
    a_down,
    tenant_of_row,
    adapter_slot,
):
    own_rows, d = tokens.shape
    half = d // CORES
    blk_count = lax.axis_size(BLK)
    grp_count = lax.axis_size("y")
    x_at, z_at, c_at, grp = (lax.axis_index(k) for k in ("x", "z", "c", "y"))
    blk = (x_at * RING + z_at) * CORES + c_at
    per_owner = a_gate.shape[0]
    tenant_count = b_gate.shape[0]
    cap = 2 * own_rows
    group_rows = own_rows * blk_count

    a_g = a_gate.reshape(per_owner * RANK, d)
    a_u = a_up.reshape(per_owner * RANK, d)
    out_f = down_output_factors.reshape(per_owner * RANK, d)
    b_g = b_gate.reshape(tenant_count * RANK, -1)
    b_u = b_up.reshape(tenant_count * RANK, -1)
    a_d = a_down.reshape(tenant_count * RANK, -1)

    all_tenants = jnp.transpose(tenant_of_row.reshape(blk_count, grp_count, own_rows), (1, 0, 2))
    all_tenants = all_tenants.reshape(grp_count, group_rows)
    hot = all_tenants[:, :, None] == jnp.arange(tenant_count, dtype=jnp.int32)
    all_slots = jnp.sum(jnp.where(hot, adapter_slot, 0), axis=2)
    all_owners = all_slots // per_owner
    at = jnp.arange(group_rows, dtype=jnp.int32)
    ahead = (all_owners[:, :, None] == all_owners[:, None, :]) & (at[:, None] > at[None, :])
    all_within = jnp.sum(ahead.astype(jnp.int32), axis=2)
    mine = all_owners == blk
    all_choose = mine[:, None, :] & (
        all_within[:, None, :] == jnp.arange(cap, dtype=jnp.int32)[None, :, None]
    )
    own_slot = jnp.sum(jnp.where(all_choose, (all_slots - per_owner * blk)[:, None, :] + 1, 0), 2) - 1
    here = lambda v: lax.dynamic_index_in_dim(v, grp, 0, keepdims=False)
    tenants, slots = here(all_tenants), here(all_slots)
    position = here(all_owners) * cap + here(all_within)
    choose = here(all_choose).astype(BF)
    rel = slots - per_owner * blk

    tall_w = jnp.concatenate([gate_weight, up_weight], axis=1)
    wide_w = jnp.concatenate([down_weight, out_f, a_g, a_u], axis=0)
    far = (1 - c_at) * half
    near = lax.ppermute(lax.dynamic_slice_in_dim(wide_w, far, half, 1), "c", SWAP)
    side = lax.ppermute(lax.dynamic_slice_in_dim(tall_w, far, half, 0), "c", SWAP)

    j = jnp.arange(group_rows, dtype=jnp.int32)
    inner = j % (CORES * own_rows)
    first, second = j // (group_rows // RING), (j // (CORES * own_rows)) % RING
    place = lambda dx, dz: (
        ((x_at + dx) % RING * RING + (z_at + dz) % RING) * CORES * own_rows + inner
    )[:, None]
    order_m, order_i = place(first, second), place(second, first)

    both = jnp.concatenate([tokens, cotangent], axis=1)
    both = lax.all_gather(both, BLK, axis=0, tiled=True)
    rel = rel[:, None]
    both, tall_w, wide_w, near, side = lax.optimization_barrier((both, tall_w, wide_w, near, side))
    pre, coef, own = project(rel, choose, both, tall_w, wide_w)
    all_own = lax.all_gather(own, "y", axis=0)
    copies = jnp.broadcast_to(coef[:, : 3 * RANK], (blk_count, cap, 3 * RANK))
    table = lax.all_to_all(copies, BLK, split_axis=0, concat_axis=0, tiled=True)
    table = jnp.pad(table.reshape(blk_count * cap, 3 * RANK), ((0, 0), (0, LANES - 3 * RANK)))
    values, placed = hidden_stage(
        tenants[:, None], position[:, None], position[None, :], table, pre, b_g, b_u, a_d
    )
    terms = placed[:, : 3 * RANK].reshape(blk_count, cap, 3 * RANK)
    terms = lax.all_to_all(terms, BLK, split_axis=0, concat_axis=0, tiled=True)
    low = jnp.sum(terms.astype(F32), axis=0).astype(BF)
    low = jnp.pad(low, ((0, 0), (0, LANES - 3 * RANK)))
    left, packed = left_stage(rel, jnp.transpose(choose), low, order_m, order_i, values)
    other = lax.ppermute(left, "c", SWAP)
    left, other, packed, all_own = lax.optimization_barrier((left, other, packed, all_own))
    packed = lax.all_gather(packed, "y", axis=0)
    pieces = products(
        c_at.reshape(1).astype(jnp.int32), left, other, tall_w, wide_w, near, side
    )
    pieces = (pieces[:3], pieces[3:])
    sent = first_step(*pieces, ("x", "z"))
    moved = second_start(*pieces, ("x", "z"), sent)
    low_all = packed[:, group_rows:, : 3 * RANK].astype(F32)
    slots_dev = per_owner // grp_count
    wanted = grp * slots_dev + jnp.arange(slots_dev, dtype=jnp.int32)
    weights = jnp.where(
        (own_slot[None] == wanted[:, None, None])[:, None],
        jnp.transpose(low_all, (2, 0, 1))[None],
        0.0,
    )
    weights = weights.reshape(slots_dev, 3, RANK, grp_count * cap)
    weights = jnp.transpose(weights, (1, 0, 2, 3)).reshape(3, slots_dev * RANK, grp_count * cap)
    weights = jnp.concatenate([weights[1], weights[2], 2.0 * weights[0]], axis=0).astype(BF)
    by_slot = slot_gradients(weights, all_own)
    tenant_dev = tenant_count // grp_count
    by_tenant = tenant_gradients(all_tenants - grp * tenant_dev, packed, tenant_dev)

    *sums, grads = second_end(*pieces, moved, *by_slot, *by_tenant)
    pieces = (in_pieces(sums[0]), in_pieces(sums[1]))
    sent = first_step(*pieces, ("z", "x"))
    moved = second_start(*pieces, ("z", "x"), sent)
    *sums, _ = second_end(*pieces, moved)
    stacked = jnp.stack([v.reshape(CORES, own_rows, half) for v in sums], axis=1)
    keep = lax.dynamic_index_in_dim(stacked, c_at, 0, keepdims=False)
    give = lax.dynamic_index_in_dim(stacked, 1 - c_at, 0, keepdims=False)
    take = lax.ppermute(give, "c", SWAP)
    result = jnp.where(
        c_at == 0,
        jnp.concatenate([keep, take], axis=2),
        jnp.concatenate([take, keep], axis=2),
    )
    return (
        result[0],
        result[1],
        *(v.reshape(slots_dev, RANK, d) for v in grads[:3]),
        *(v.reshape(tenant_dev, RANK, -1) for v in grads[3:]),
    )


def solution(mesh):
    cut = Mesh(mesh.devices.reshape(RING, RING, CORES, mesh.shape["grp"]), ("x", "z", "c", "y"))
    every = (*BLK, "y")
    return jax.shard_map(
        local,
        mesh=cut,
        in_specs=(
            P(every, None),
            P(every, None),
            P(None, BLK),
            P(None, BLK),
            P(BLK, None),
            P(BLK, None, None),
            P(BLK, None, None),
            P(BLK, None, None),
            P(None, None, BLK),
            P(None, None, BLK),
            P(None, None, BLK),
            P(),
            P(),
        ),
        out_specs=(
            P(every, None),
            P(every, None),
            P(every, None, None),
            P(every, None, None),
            P(every, None, None),
            P("y", None, BLK),
            P("y", None, BLK),
            P("y", None, BLK),
        ),
        check_vma=False,
    )
```
